32 devices in a mesh: head: 4 (over x, core), tensor: 4 (over z), dp: 2 (over y).
Axes of the slice: x: 2, y: 2, z: 4, core: 2. Of those that a mesh axis runs over, the one named last changes fastest.
Arguments:
- trunk_hidden: bfloat16 [96, 5120], P('dp', 'tensor'), may hold values from -60 to 60
- next_embeds: bfloat16 [4, 96, 5120], P('head', 'dp', 'tensor'), may hold values from -6 to 6
- combine_weight: bfloat16 [4, 10240, 5120], P('head', 'dp', 'tensor'), may hold values from -0.0625 to 0.0625
- final_gain: float32 [5120], P('tensor'), may hold values from 0.5 to 1.5
- unembed_weight: bfloat16 [16384, 5120], P('dp', 'tensor'), may hold values from -32 to 32
- target_ids: int32 [4, 96], P('head'), may hold values from 0 to 16383
- loss_scale: float32 [4, 96], P('head'), may hold values from 2 to 32
Outputs:
- trunk_grad: float32 [96, 5120], P('dp', 'tensor')
- embed_grad: float32 [4, 96, 5120], P('head', 'dp', 'tensor')
- combine_grad: float32 [4, 10240, 5120], P('head', 'dp', 'tensor')
- unembed_grad: float32 [2, 4, 2048, 5120], P('dp', 'head', None, 'tensor')
The draws below stay inside these ranges and needn't reach their ends.
All inputs are finite; a program needn't handle non-finite values.
Results may differ from the reference program's by a relative error of at most 0.02.
Values may be sent and summed in bfloat16 or wider, within the bound.
No kernel may reach another device: no remote copies, remote signals or barrier semaphores. Data moves between devices by JAX's collectives and lax.ppermute only.
A program may use at most 192 MiB of HBM per device.

```python
import math
import jax
import jax.numpy as jnp
import numpy as np
from jax import lax

D = 5120
VOCAB = 16384
TOKENS = 96
HEADS = 4
N_DP = 2


def shared_direction(key):
    return jax.random.normal(jax.random.fold_in(key, 7001), (D,), jnp.float32)


def draw_trunk_hidden(key, part):
    noise = jax.random.normal(jax.random.fold_in(key, 11), (TOKENS, D), jnp.float32)
    values = noise
    chosen = jax.random.randint(jax.random.fold_in(key, 13), (8,), 0, TOKENS)
    direction = shared_direction(key)
    aligned = 6.0 * direction[None, :] + 0.3 * jax.random.normal(jax.random.fold_in(key, 14), (8, D), jnp.float32)
    values = values.at[chosen].set(aligned)
    return jnp.clip(values, -60.0, 60.0).astype(jnp.bfloat16)


def draw_unembed_weight(key, part):
    sigma = 3.0 / math.sqrt(D)
    values = sigma * jnp.clip(jax.random.normal(jax.random.fold_in(key, 24), (VOCAB, D), jnp.float32), -6.0, 6.0)
    direction = shared_direction(key)
    chosen = jax.random.permutation(jax.random.fold_in(key, 22), VOCAB)[:6]
    strength = jnp.array([150.0, 148.0, 260.0, 258.0, 380.0, 378.0], jnp.float32)
    extra = 0.5 / math.sqrt(D) * jax.random.normal(jax.random.fold_in(key, 23), (6, D), jnp.float32)
    aligned = strength[:, None] * direction[None, :] / D + extra
    values = values.at[chosen].set(aligned)
    return jnp.clip(values, -32.0, 32.0).astype(jnp.bfloat16)


def touch_ends(result, rng, low, high):
    shape = result.shape
    spot = [jax.random.randint(jax.random.fold_in(rng, axis), (), 0, shape[axis]) for axis in range(len(shape))]
    result = result.at[tuple(spot)].set(low)
    longest = shape.index(max(shape))
    spot[longest] = (spot[longest] + 1) % shape[longest]
    return result.at[tuple(spot)].set(high)


def shard_levels(stream_key, extent, cuts, least, high):
    factor_of = 1.0
    for axis_at, parts in cuts:
        heights = jax.random.uniform(jax.random.fold_in(jax.random.fold_in(stream_key, 6), axis_at), (parts,), jnp.float32, least / len(cuts), high / len(cuts))
        factor_of = factor_of * jnp.repeat(jnp.exp(heights), extent[axis_at] // parts).reshape((-1,) + (1,) * (len(extent) - 1 - axis_at))
    return factor_of


def rank_table(count, slope):
    portions = [(1 << 20) // math.isqrt(standing ** slope) + 1 for standing in range(1, count + 1)]
    width = 1 + sum(portions) // (1 << 30)
    return np.cumsum(np.array([max(1, weight // width) for weight in portions]))


def ranked(stream_key, shape, number_of, skew):
    table = rank_table(number_of, skew)
    lot = jax.random.randint(jax.random.fold_in(stream_key, 1), shape, 0, int(table[number_of - 1]))
    standing = jnp.searchsorted(jnp.asarray(table, jnp.int32), lot, side="right")
    return jax.random.permutation(jax.random.fold_in(stream_key, 2), number_of)[standing].astype(jnp.int32)


def bell_draw(key, shape, spread, bound, pieces=(), held_as=jnp.bfloat16):
    loudness = shard_levels(key, shape, pieces, -0.22, 0.18) if pieces else 1.0
    values = jax.random.normal(key, shape, jnp.float32) * spread * loudness
    return jnp.minimum(jnp.maximum(values, -bound), bound).astype(held_as)


def setup_inputs(seed: int = 0) -> dict:
    streams_of = jax.random.split(jax.random.key(seed), 8)
    return {
        "trunk_hidden": draw_trunk_hidden(jax.random.fold_in(streams_of[7], 71), 0),
        "next_embeds": bell_draw(streams_of[1], (HEADS, TOKENS, D), 1.0, 6.0, ((0, 4), (1, 2), (2, 4))),
        "combine_weight": bell_draw(streams_of[2], (HEADS, 2 * D, D), (2 * D) ** -0.5, 0.0625, ((0, 4), (1, 2), (2, 4))),
        "final_gain": jnp.clip(1.0 + 0.1 * jax.random.normal(streams_of[3], (D,), jnp.float32), 0.5, 1.5),
        "unembed_weight": draw_unembed_weight(jax.random.fold_in(streams_of[7], 71), 0),
        "target_ids": touch_ends(ranked(streams_of[5], (HEADS, TOKENS), VOCAB, 2), jax.random.fold_in(streams_of[5], 3), 0, VOCAB - 1).astype(jnp.int32),
        "loss_scale": jnp.clip(jnp.exp(math.log(32.0) - 2.7725887 * jax.random.uniform(streams_of[6], (HEADS, TOKENS), jnp.float32) ** shard_levels(streams_of[6], (HEADS, TOKENS), ((0, 4),), -0.2, 0.2)), 2.0, 32.0),
    }


epsilon = 1e-05

def contract_rows(left, right):
    return lax.dot_general(left, right, (((0,), (0,)), ((), ())), preferred_element_type=jnp.float32)

def contract_cols(left, right):
    return lax.dot_general(left, right, (((1,), (1,)), ((), ())), preferred_element_type=jnp.float32)

def reference(trunk_hidden, next_embeds, combine_weight, final_gain, unembed_weight, target_ids, loss_scale):
    trunk_float = trunk_hidden.astype(jnp.float32)
    trunk_scale = lax.rsqrt(lax.optimization_barrier(jnp.sum(trunk_float * trunk_float, axis=1)) / D + epsilon)
    trunk_normed = trunk_float * trunk_scale[:, None]
    vocab_ids = lax.broadcasted_iota(jnp.int32, (1, VOCAB), 1)
    unembed_total = jnp.zeros((VOCAB, D), jnp.float32)
    trunk_total = jnp.zeros((TOKENS, D), jnp.float32)
    embed_list = []
    combine_list = []
    for which_head in range(HEADS):
        embed_float = next_embeds[which_head].astype(jnp.float32)
        embed_scale = lax.rsqrt(lax.optimization_barrier(jnp.sum(embed_float * embed_float, axis=1)) / D + epsilon)
        embed_normed = embed_float * embed_scale[:, None]
        joined = jnp.concatenate([trunk_normed.astype(jnp.bfloat16), embed_normed.astype(jnp.bfloat16)], axis=1)
        mixed = trunk_float + jnp.dot(joined, combine_weight[which_head], preferred_element_type=jnp.float32)
        mixed_scale = lax.rsqrt(lax.optimization_barrier(jnp.sum(mixed * mixed, axis=1)) / D + epsilon)
        mixed_normed = mixed * mixed_scale[:, None]
        normed_out = (mixed_normed * final_gain[None, :]).astype(jnp.bfloat16)
        logits = contract_cols(normed_out, unembed_weight)
        largest = lax.optimization_barrier(jnp.max(logits, axis=1, keepdims=True))
        shifted = jnp.exp(logits - largest)
        probs = shifted / lax.optimization_barrier(jnp.sum(shifted, axis=1, keepdims=True))
        hits = (vocab_ids == target_ids[which_head][:, None]).astype(jnp.float32)
        grad_logits = (loss_scale[which_head][:, None] * (probs - hits)).astype(jnp.bfloat16)
        grad_normed = jnp.dot(grad_logits, unembed_weight, preferred_element_type=jnp.float32)
        vocab_term = lax.optimization_barrier(contract_rows(grad_logits, normed_out).astype(jnp.bfloat16))
        unembed_total = unembed_total + vocab_term.astype(jnp.float32)
        scaled_grad = grad_normed * final_gain[None, :]
        grad_dots = lax.optimization_barrier(jnp.sum(scaled_grad * mixed_normed, axis=1)) / D
        grad_mixed = mixed_scale[:, None] * (scaled_grad - mixed_normed * grad_dots[:, None])
        grad_mixed_low = grad_mixed.astype(jnp.bfloat16)
        combine_list.append(contract_rows(joined, grad_mixed_low))
        joined_grad = contract_cols(grad_mixed_low, combine_weight[which_head])
        trunk_side = joined_grad[:, :D]
        embed_side = joined_grad[:, D:]
        trunk_dots = lax.optimization_barrier(jnp.sum(trunk_side * trunk_normed, axis=1)) / D
        embed_dots = lax.optimization_barrier(jnp.sum(embed_side * embed_normed, axis=1)) / D
        embed_list.append(embed_scale[:, None] * (embed_side - embed_normed * embed_dots[:, None]))
        trunk_total = trunk_total + grad_mixed + trunk_scale[:, None] * (trunk_side - trunk_normed * trunk_dots[:, None])
    unembed_grad = unembed_total.reshape(N_DP, HEADS, VOCAB // (N_DP * HEADS), D)
    return (trunk_total, jnp.stack(embed_list), jnp.stack(combine_list), unembed_grad)
```

```python
import jax
import jax.numpy as jnp
from jax import lax
from jax.sharding import PartitionSpec as P

epsilon = 1e-05
f32 = jnp.float32
bf16 = jnp.bfloat16


def contract_rows(left, right):
    return lax.dot_general(
        left, right, (((0,), (0,)), ((), ())), preferred_element_type=f32
    )


def contract_cols(left, right):
    return lax.dot_general(
        left, right, (((1,), (1,)), ((), ())), preferred_element_type=f32
    )


def plain_dot(left, right):
    return jnp.dot(left, right, preferred_element_type=f32)


def shift(value, axis, size, by):
    return lax.ppermute(value, axis, [(i, (i + by) % size) for i in range(size)])


def flip(value, axis, size, mask):
    return lax.ppermute(value, axis, [(i, i ^ mask) for i in range(size)])


def swap(value):
    return lax.ppermute(value, "dp", [(0, 1), (1, 0)])


def fast_local(
    n_head,
    n_tensor,
    trunk_hidden,
    next_embeds,
    combine_weight,
    final_gain,
    unembed_weight,
    target_ids,
    loss_scale,
):
    half, width = trunk_hidden.shape
    rows = 2 * half
    features = width * n_tensor
    weight_block = combine_weight[0]
    vocab_part = unembed_weight.shape[0]
    piece = vocab_part // n_tensor
    d = lax.axis_index("dp")
    t = lax.axis_index("tensor")
    h = lax.axis_index("head")
    first = d == 0
    targets = target_ids[0]
    row_weights = loss_scale[0]

    def combine_rows(which):
        return lax.dynamic_slice_in_dim(weight_block, which * width, width, 0)

    def vocab_rows(which):
        return lax.dynamic_slice_in_dim(unembed_weight, which * piece, piece, 0)

    def around(by):
        return lax.rem(t + by + n_tensor, n_tensor)

    def spread(value):
        return [value] + [shift(value, "tensor", n_tensor, r) for r in range(1, n_tensor)]

    with jax.named_scope("inputs"):
        embeds = next_embeds[0]
        other = swap(jnp.where(first, embeds, trunk_hidden))
        kept = jnp.where(first, trunk_hidden, embeds)
        trunk_other = swap(trunk_hidden)
        trunk_rows = jnp.concatenate(
            [jnp.where(first, trunk_hidden, trunk_other), jnp.where(first, trunk_other, trunk_hidden)], axis=0
        ).astype(f32)
        own = jnp.concatenate(
            [jnp.where(first, kept, other), jnp.where(first, other, kept)], axis=0
        )
        parts = spread(own)
    with jax.named_scope("projection"):
        square_sum = sum(jnp.sum(jnp.square(p.astype(f32)), axis=1) for p in parts)
        in_scale = lax.rsqrt(square_sum / features + epsilon)
        raw = sum(plain_dot(p, combine_rows(around(-r))) for r, p in enumerate(parts))
        projected = raw * in_scale[:, None]
        mixed = trunk_rows + (projected + swap(projected.astype(bf16)).astype(f32))
        gained = mixed * final_gain[None, :]
        low = gained.astype(bf16)
    with jax.named_scope("mixed_scale"):
        mixed_sums = sum(spread(jnp.sum(mixed * mixed, axis=1)))
        mixed_scale = lax.rsqrt(mixed_sums / features + epsilon)
        normed_out = (gained * mixed_scale[:, None]).astype(bf16)
        normed_heads = [normed_out] + [
            flip(normed_out, "head", n_head, m) for m in range(1, n_head)
        ]
    with jax.named_scope("logits"):
        table = jnp.array([[3, 2, 1, 0], [3, 2, 0, 1], [0, 1, 3, 2], [0, 1, 2, 3]], jnp.int32)
        order = table[t]
        slots = [contract_cols(low, vocab_rows(order[j])) for j in range(4)]
        one = lax.ppermute(slots[0], "tensor", [(0, 1), (3, 2)])
        two = jnp.where((t == 0) | (t == 3), slots[1], slots[0] + one)
        right = lax.ppermute(two, "tensor", [(0, 1), (1, 2)])
        left = lax.ppermute(two, "tensor", [(3, 2), (2, 1)])
        right = jnp.where(t == 1, slots[1], slots[2]) + right
        left = jnp.where(t == 2, slots[1], slots[2]) + left
        right = lax.ppermute(right, "tensor", [(0, 1), (1, 2), (2, 3)])
        left = lax.ppermute(left, "tensor", [(3, 2), (2, 1), (1, 0)])
        logits = (slots[3] + right + left) * mixed_scale[:, None]
    with jax.named_scope("softmax"):
        ids = lax.broadcasted_iota(jnp.int32, (1, piece), 1) + d * vocab_part
        hits = (ids + t * piece) == targets[:, None]
        top = jnp.max(logits, axis=1)
        shifted = jnp.exp(logits - top[:, None])
        total = jnp.sum(shifted, axis=1)
        at_target = jnp.sum(jnp.where(hits, logits, 0.0), axis=1)
        stats = spread(jnp.stack([top, total, at_target]))
        shifted_low = shifted.astype(bf16)
        shifted_parts = spread(shifted_low)
        tops = [s[0] for s in stats]
        part_top = jnp.max(jnp.stack(tops), axis=0)
        part_sum = sum(s[1] * jnp.exp(s[0] - part_top) for s in stats)
        part_hit = sum(s[2] for s in stats)
        there = swap(jnp.stack([part_top, part_sum, part_hit]))
        largest = jnp.maximum(part_top, there[0])
        summed = part_sum * jnp.exp(part_top - largest) + there[1] * jnp.exp(there[0] - largest)
        hit_grad = row_weights * (jnp.exp(part_hit + there[2] - largest) / summed - 1.0)
        grads = []
        for r, e in enumerate(shifted_parts):
            factor = row_weights * jnp.exp(tops[r] - largest) / summed
            mine = (ids + around(-r) * piece) == targets[:, None]
            grads.append(
                jnp.where(mine, hit_grad[:, None], e.astype(f32) * factor[:, None]).astype(bf16)
            )
        dots_part = sum(spread(jnp.sum(grads[0].astype(f32) * logits, axis=1)))
        grad_dots = dots_part + swap(dots_part)
    with jax.named_scope("grad_normed"):
        grad_part = sum(plain_dot(g, vocab_rows(around(-r))) for r, g in enumerate(grads))
        grad_normed = grad_part + swap(grad_part.astype(bf16)).astype(f32)
        mixed_normed = mixed * mixed_scale[:, None]
        grad_mixed = mixed_scale[:, None] * (
            grad_normed * final_gain[None, :] - mixed_normed * (grad_dots / features)[:, None]
        )
        grad_low = grad_mixed.astype(bf16)
    with jax.named_scope("joined_grad"):
        dots = sum(spread(jnp.sum(grad_low.astype(f32) * projected, axis=1)))
        side = [
            shift(contract_cols(grad_low, combine_rows(around(r))).astype(bf16), "tensor", n_tensor, r)
            for r in range(1, n_tensor)
        ]
        side = contract_cols(grad_low, combine_rows(t)) + sum(s.astype(f32) for s in side)
        own_normed = own.astype(f32) * in_scale[:, None]
        term = in_scale[:, None] * (side - own_normed * (dots / features)[:, None])
        term = jnp.where(first, term + grad_mixed, term)
        theirs = swap(jnp.where(first, term[half:], term[:half]).astype(bf16)).astype(f32)
        embed_grad = jnp.where(first, theirs, term[half:])[None]
        trunk_sum = jnp.where(first, term[:half], theirs)
        mask = 1
        while mask < n_head:
            trunk_low = trunk_sum.astype(bf16)
            trunk_sum = trunk_low.astype(f32) + flip(trunk_low, "head", n_head, mask).astype(f32)
            mask *= 2
        trunk_grad = trunk_sum
    with jax.named_scope("combine_grad"):
        stacked = jnp.stack(parts)
        ordered = jnp.concatenate(
            [
                lax.dynamic_index_in_dim(stacked, around(-c), 0, keepdims=False)
                for c in range(n_tensor)
            ],
            axis=1,
        )
        combine_grad = contract_rows(ordered, (in_scale[:, None] * grad_mixed).astype(bf16))[None]
    with jax.named_scope("unembed_grad"):
        grad_stack = jnp.stack(grads)
        grad_heads = []
        for m in range(n_head):
            piece_of = lax.dynamic_index_in_dim(
                grad_stack, around(-(h ^ m)), 0, keepdims=False
            )
            grad_heads.append(flip(piece_of, "head", n_head, m) if m else piece_of)
        unembed_grad = contract_rows(
            jnp.concatenate(grad_heads, axis=0), jnp.concatenate(normed_heads, axis=0)
        )
        unembed_grad = unembed_grad.reshape(1, 1, piece, width)
    return (trunk_grad, embed_grad, combine_grad, unembed_grad)


def general_local(
    n_tensor,
    trunk_hidden,
    next_embeds,
    combine_weight,
    final_gain,
    unembed_weight,
    target_ids,
    loss_scale,
):
    rows, part_width = trunk_hidden.shape
    features = part_width * n_tensor
    vocab_part = unembed_weight.shape[0]
    weight_block = combine_weight[0]
    trunk_whole, embed_whole = (
        lax.all_gather(trunk_hidden, "tensor", axis=1, tiled=True),
        lax.all_gather(next_embeds[0], "tensor", axis=1, tiled=True),
    )
    trunk_float = trunk_whole.astype(f32)
    embed_float = embed_whole.astype(f32)
    trunk_scale = lax.rsqrt(jnp.sum(trunk_float * trunk_float, axis=1) / features + epsilon)
    embed_scale = lax.rsqrt(jnp.sum(embed_float * embed_float, axis=1) / features + epsilon)
    trunk_normed = trunk_float * trunk_scale[:, None]
    embed_normed = embed_float * embed_scale[:, None]
    joined = jnp.concatenate([trunk_normed.astype(bf16), embed_normed.astype(bf16)], axis=1)
    feature_start = lax.axis_index("tensor") * part_width
    trunk_local = lax.dynamic_slice_in_dim(trunk_normed, feature_start, part_width, 1)
    embed_local = lax.dynamic_slice_in_dim(embed_normed, feature_start, part_width, 1)
    blocks = lax.all_to_all(joined, "dp", split_axis=1, concat_axis=0, tiled=True)
    projected = lax.psum_scatter(
        plain_dot(blocks, weight_block).astype(bf16), "dp", scatter_dimension=0, tiled=True
    ).astype(f32)
    mixed = trunk_hidden.astype(f32) + projected
    mixed_sums = lax.psum(jnp.sum(mixed * mixed, axis=1), "tensor")
    mixed_scale = lax.rsqrt(mixed_sums / features + epsilon)
    mixed_normed = mixed * mixed_scale[:, None]
    normed_out = (mixed_normed * final_gain[None, :]).astype(bf16)
    normed_all = lax.all_gather(normed_out, "dp", axis=0, tiled=True)
    logits = lax.psum(contract_cols(normed_all, unembed_weight), "tensor")
    largest = lax.pmax(jnp.max(logits, axis=1), "dp")
    shifted = jnp.exp(logits - largest[:, None])
    summed = lax.psum(jnp.sum(shifted, axis=1), "dp")
    probs = shifted / summed[:, None]
    vocab_ids = (
        lax.broadcasted_iota(jnp.int32, (1, vocab_part), 1) + lax.axis_index("dp") * vocab_part
    )
    hits = (vocab_ids == target_ids[0][:, None]).astype(f32)
    grad_local = (loss_scale[0][:, None] * (probs - hits)).astype(bf16)
    grad_normed = lax.psum_scatter(
        plain_dot(grad_local, unembed_weight).astype(bf16), "dp", scatter_dimension=0, tiled=True
    ).astype(f32)
    vocab_term = contract_rows(grad_local, normed_all).astype(bf16)
    vocab_total = lax.psum_scatter(vocab_term, "head", scatter_dimension=0, tiled=True).astype(f32)
    unembed_grad = vocab_total.reshape(1, 1, vocab_total.shape[0], part_width)
    scaled_grad = grad_normed * final_gain[None, :]
    grad_dots = lax.psum(jnp.sum(scaled_grad * mixed_normed, axis=1), "tensor")
    grad_mixed = mixed_scale[:, None] * (
        scaled_grad - mixed_normed * (grad_dots / features)[:, None]
    )
    grad_all = lax.all_gather(grad_mixed.astype(bf16), "dp", axis=0, tiled=True)
    combine_grad = contract_rows(blocks, grad_all)[None]
    joined_part = lax.all_to_all(
        contract_cols(grad_all, weight_block).astype(bf16),
        "dp",
        split_axis=0,
        concat_axis=1,
        tiled=True,
    )
    joined_grad = lax.psum_scatter(
        joined_part.reshape(rows, 2, features), "tensor", scatter_dimension=2, tiled=True
    ).astype(f32)
    trunk_side = joined_grad[:, 0]
    embed_side = joined_grad[:, 1]
    trunk_dots, embed_dots = lax.psum(
        (jnp.sum(trunk_side * trunk_local, axis=1), jnp.sum(embed_side * embed_local, axis=1)),
        "tensor",
    )
    trunk_term = trunk_scale[:, None] * (
        trunk_side - trunk_local * (trunk_dots / features)[:, None]
    )
    embed_grad = (
        embed_scale[:, None] * (embed_side - embed_local * (embed_dots / features)[:, None])
    )[None]
    trunk_grad = lax.psum((grad_mixed + trunk_term).astype(bf16), "head").astype(f32)
    return (trunk_grad, embed_grad, combine_grad, unembed_grad)


def solution(mesh):
    n_head, n_tensor, n_dp = mesh.shape["head"], mesh.shape["tensor"], mesh.shape["dp"]
    in_specs = (
        P("dp", "tensor"),
        P("head", "dp", "tensor"),
        P("head", "dp", "tensor"),
        P("tensor"),
        P("dp", "tensor"),
        P("head", None),
        P("head", None),
    )
    out_specs = (
        P("dp", "tensor"),
        P("head", "dp", "tensor"),
        P("head", "dp", "tensor"),
        P("dp", "head", None, "tensor"),
    )
    if n_dp == 2 and n_tensor == 4 and n_head == 4:

        def local(*args):
            return fast_local(n_head, n_tensor, *args)

    else:

        def local(*args):
            return general_local(n_tensor, *args)

    return jax.shard_map(local, mesh=mesh, in_specs=in_specs, out_specs=out_specs, check_vma=False)
```

```python
import jax
import jax.numpy as jnp
from jax import lax
from jax.experimental import pallas as pl
from jax.experimental.pallas import tpu as pltpu
from jax.sharding import PartitionSpec as P

epsilon = 1e-05
f32 = jnp.float32
bf16 = jnp.bfloat16
kernel_memory = 12 << 20
stream_memory = 44 << 20
brief = pl.CostEstimate(flops=0, bytes_accessed=0, transcendentals=0)


def contract_rows(left, right):
    return lax.dot_general(
        left, right, (((0,), (0,)), ((), ())), preferred_element_type=f32
    )


def contract_cols(left, right):
    return lax.dot_general(
        left, right, (((1,), (1,)), ((), ())), preferred_element_type=f32
    )


def plain_dot(left, right):
    return jnp.dot(left, right, preferred_element_type=f32)


def shift(value, axis, size, by):
    return lax.ppermute(value, axis, [(i, (i + by) % size) for i in range(size)])


def flip(value, axis, size, mask):
    return lax.ppermute(value, axis, [(i, i ^ mask) for i in range(size)])


def swap(value):
    return lax.ppermute(value, "dp", [(0, 1), (1, 0)])


def chunk_copy(weight, which, size, block, held, done, j):
    start = pl.multiple_of(which[0] * size + j * block, block)
    return pltpu.make_async_copy(weight.at[pl.ds(start, block)], held.at[j], done.at[j])


def stream_columns_kernel(which, left, weight, out, held, done):
    blocks, block, _ = held.shape
    copies = [
        chunk_copy(weight, which, blocks * block, block, held, done, j) for j in range(blocks)
    ]
    for copy in copies:
        copy.start()
    for j, copy in enumerate(copies):
        copy.wait()
        out[:, j * block : (j + 1) * block] = contract_cols(left[...], held[j]).astype(out.dtype)


def stream_rows_kernel(which, left, weight, out, held, done):
    blocks, block, _ = held.shape
    copies = [
        chunk_copy(weight, which, blocks * block, block, held, done, j) for j in range(blocks)
    ]
    for copy in copies:
        copy.start()
    for j, copy in enumerate(copies):
        copy.wait()
        product = plain_dot(left[:, j * block : (j + 1) * block], held[j])
        if j == 0:
            out[...] = product
        else:
            out[...] += product


def stream(kernel, left, weight, which, size, out_width, blocks):
    rows = left.shape[0]
    width = weight.shape[1]
    block = size // blocks
    return pl.pallas_call(
        kernel,
        out_shape=jax.ShapeDtypeStruct((rows, out_width), f32),
        in_specs=[
            pl.BlockSpec(memory_space=pltpu.SMEM),
            pl.BlockSpec(memory_space=pltpu.VMEM),
            pl.BlockSpec(memory_space=pl.ANY),
        ],
        out_specs=pl.BlockSpec(memory_space=pltpu.VMEM),
        scratch_shapes=[
            pltpu.VMEM((blocks, block, width), weight.dtype),
            pltpu.SemaphoreType.DMA((blocks,)),
        ],
        compiler_params=pltpu.CompilerParams(vmem_limit_bytes=stream_memory),
        cost_estimate=brief,
    )(which.reshape(1), left, weight)


def stream_columns(left, weight, which, size, blocks):
    return stream(stream_columns_kernel, left, weight, which, size, size, blocks)


def stream_rows(left, weight, which, blocks):
    return stream(
        stream_rows_kernel, left, weight, which, left.shape[1], weight.shape[1], blocks
    )


def dot_columns_kernel(which, left, right, out):
    out[...] = contract_cols(left[...], right[...]).astype(out.dtype)


def dot_columns(left, weight, which, size, blocks, dtype):
    rows, depth = left.shape
    block = size // blocks
    return pl.pallas_call(
        dot_columns_kernel,
        out_shape=jax.ShapeDtypeStruct((rows, size), dtype),
        grid_spec=pltpu.PrefetchScalarGridSpec(
            num_scalar_prefetch=1,
            grid=(blocks,),
            in_specs=[
                pl.BlockSpec((rows, depth), lambda j, c: (0, 0)),
                pl.BlockSpec((block, depth), lambda j, c: (c[0] * blocks + j, 0)),
            ],
            out_specs=pl.BlockSpec((rows, block), lambda j, c: (0, j)),
        ),
        compiler_params=pltpu.CompilerParams(vmem_limit_bytes=kernel_memory),
        cost_estimate=brief,
    )(which.reshape(1), left, weight)


def dot_columns_apart_kernel(which, left, right, extra, *outs):
    size = right.shape[0]
    for k, out in enumerate(outs):

        @pl.when(pl.program_id(0) == k)
        def _():
            out[:, :size] = contract_cols(left[...], right[...]).astype(out.dtype)
            out[:, size:] = extra[...]


def dot_columns_apart(left, weight, which, size, extra):
    rows, depth = left.shape
    wide = size + extra.shape[1]
    return pl.pallas_call(
        dot_columns_apart_kernel,
        out_shape=[jax.ShapeDtypeStruct((rows, wide), bf16) for _ in which],
        grid_spec=pltpu.PrefetchScalarGridSpec(
            num_scalar_prefetch=1,
            grid=(len(which),),
            in_specs=[
                pl.BlockSpec((rows, depth), lambda i, c: (0, 0)),
                pl.BlockSpec((size, depth), lambda i, c: (c[i], 0)),
                pl.BlockSpec(extra.shape, lambda i, c: (0, 0)),
            ],
            out_specs=[pl.BlockSpec((rows, wide), lambda i, c: (0, 0)) for _ in which],
        ),
        compiler_params=pltpu.CompilerParams(vmem_limit_bytes=kernel_memory),
        cost_estimate=brief,
    )(jnp.stack(which), left, weight, extra)


def dot_rows_kernel(which, left, right, out):
    product = plain_dot(left[...], right[...])

    @pl.when(pl.program_id(0) == 0)
    def _():
        out[...] = product

    @pl.when(pl.program_id(0) > 0)
    def _():
        out[...] += product


def dot_rows_onto_kernel(which, left, right, base, out):
    product = plain_dot(left[...], right[...])

    @pl.when(pl.program_id(0) == 0)
    def _():
        out[...] = base[...] + product

    @pl.when(pl.program_id(0) > 0)
    def _():
        out[...] += product


def dot_rows(left, weight, which, blocks, base=None):
    rows, size = left.shape
    width = weight.shape[1]
    block = size // blocks
    whole = pl.BlockSpec((rows, width), lambda j, c: (0, 0))
    return pl.pallas_call(
        dot_rows_kernel if base is None else dot_rows_onto_kernel,
        out_shape=jax.ShapeDtypeStruct((rows, width), f32),
        grid_spec=pltpu.PrefetchScalarGridSpec(
            num_scalar_prefetch=1,
            grid=(blocks,),
            in_specs=[
                pl.BlockSpec((rows, block), lambda j, c: (0, j)),
                pl.BlockSpec((block, width), lambda j, c: (c[0] * blocks + j, 0)),
            ]
            + ([] if base is None else [whole]),
            out_specs=whole,
        ),
        compiler_params=pltpu.CompilerParams(vmem_limit_bytes=kernel_memory),
        cost_estimate=brief,
    )(which.reshape(1), left, weight, *([] if base is None else [base]))


def combine_kernel(which, part, grad, out):
    out[...] = contract_rows(part[0], grad[...])


def combine_rows(parts, grad, order, blocks):
    count, rows, width = parts.shape
    block = width // blocks
    return pl.pallas_call(
        combine_kernel,
        out_shape=jax.ShapeDtypeStruct((count * width, grad.shape[1]), f32),
        grid_spec=pltpu.PrefetchScalarGridSpec(
            num_scalar_prefetch=1,
            grid=(count, blocks),
            in_specs=[
                pl.BlockSpec((1, rows, block), lambda c, j, w: (w[c], 0, j)),
                pl.BlockSpec((rows, grad.shape[1]), lambda c, j, w: (0, 0)),
            ],
            out_specs=pl.BlockSpec((block, grad.shape[1]), lambda c, j, w: (c * blocks + j, 0)),
        ),
        compiler_params=pltpu.CompilerParams(vmem_limit_bytes=kernel_memory),
        cost_estimate=brief,
    )(order, parts, grad)


def head_sum_kernel(*refs):
    out = refs[-1]
    count = (len(refs) - 1) // 2
    left = jnp.concatenate([r[...] for r in refs[:count]], axis=0)
    right = jnp.concatenate([r[...] for r in refs[count : 2 * count]], axis=0)
    out[...] = contract_rows(left, right)


def head_sum(grads, normed, blocks):
    rows, size = grads[0].shape
    width = normed[0].shape[1]
    block = size // blocks
    return pl.pallas_call(
        head_sum_kernel,
        out_shape=jax.ShapeDtypeStruct((size, width), f32),
        grid=(blocks,),
        in_specs=[pl.BlockSpec((rows, block), lambda j: (0, j))] * len(grads)
        + [pl.BlockSpec((rows, width), lambda j: (0, 0))] * len(normed),
        out_specs=pl.BlockSpec((block, width), lambda j: (j, 0)),
        compiler_params=pltpu.CompilerParams(vmem_limit_bytes=kernel_memory),
        cost_estimate=brief,
    )(*grads, *normed)


def fast_local(
    n_head,
    n_tensor,
    trunk_hidden,
    next_embeds,
    combine_weight,
    final_gain,
    unembed_weight,
    target_ids,
    loss_scale,
):
    half, width = trunk_hidden.shape
    features = width * n_tensor
    weight_block = combine_weight[0]
    vocab_part = unembed_weight.shape[0]
    piece = vocab_part // n_tensor
    d = lax.axis_index("dp")
    t = lax.axis_index("tensor")
    h = lax.axis_index("head")
    first = d == 0
    targets = target_ids[0]
    row_weights = loss_scale[0]

    def spread(value):
        return [value] + [flip(value, "tensor", n_tensor, r) for r in range(1, n_tensor)]

    with jax.named_scope("inputs"):
        embeds = next_embeds[0]
        kept = jnp.where(first, trunk_hidden, embeds)
        given = jnp.where(first, embeds, trunk_hidden)
        kept_parts = spread(kept)
        swapped = swap(jnp.concatenate([given, trunk_hidden], axis=0))
        kept_parts, swapped = lax.optimization_barrier((kept_parts, swapped))
        given_parts = spread(swapped[:half])

        def all_rows(k, g):
            return jnp.concatenate([jnp.where(first, k, g), jnp.where(first, g, k)], axis=0)

        own = all_rows(kept_parts[0], given_parts[0])
        raw = dot_rows(own, weight_block, t, 2)
        given_parts, raw = lax.optimization_barrier((given_parts, raw))
        parts = [own] + [all_rows(k, g) for k, g in zip(kept_parts[1:], given_parts[1:])]
        trunk_rows = jnp.where(
            first, own, jnp.concatenate([swapped[half:], trunk_hidden], axis=0)
        ).astype(f32)
    with jax.named_scope("projection"):
        square_sum = sum(jnp.sum(jnp.square(p.astype(f32)), axis=1) for p in parts)
        in_scale = lax.rsqrt(square_sum / features + epsilon)
        for r in range(1, n_tensor):
            raw = dot_rows(parts[r], weight_block, t ^ r, 2, raw)
        projected = raw * in_scale[:, None]
        mixed = trunk_rows + (projected + swap(projected.astype(bf16)).astype(f32))
        gained = mixed * final_gain[None, :]
        low = gained.astype(bf16)
    with jax.named_scope("logits"):
        far = stream_columns(low, unembed_weight, t ^ 3, piece, 4)
        ends = lax.ppermute(far, "tensor", [(0, 1), (3, 2)])
        middle = lax.ppermute(far, "tensor", [(1, 2), (2, 1)])
        mixed_squares = spread(jnp.sum(mixed * mixed, axis=1))
        cross, near, last = [
            stream_columns(low, unembed_weight, t ^ r, piece, 4) for r in (2, 1, 0)
        ]
        wanted = targets - d * vocab_part
        ends, middle, mixed_squares, cross, near, last, wanted = lax.optimization_barrier(
            (ends, middle, mixed_squares, cross, near, last, wanted)
        )
        mixed_scale = lax.rsqrt(sum(mixed_squares) / features + epsilon)
        normed_out = (gained * mixed_scale[:, None]).astype(bf16)
        normed_heads = [normed_out] + [
            flip(normed_out, "head", n_head, m) for m in range(1, n_head)
        ]
        cross = flip(cross + ends, "tensor", n_tensor, 2)
        near = flip(near, "tensor", n_tensor, 1)
        chosen = lax.broadcasted_iota(jnp.int32, (1, vocab_part), 1) == wanted[:, None]
        target_rows = stream_rows(chosen.astype(bf16), unembed_weight, jnp.int32(0), 16)
        cross, near, normed_heads, target_rows = lax.optimization_barrier(
            (cross, near, normed_heads, target_rows)
        )
        logits = (last + middle + cross + near) * mixed_scale[:, None]
        mixed_normed = mixed * mixed_scale[:, None]
    with jax.named_scope("softmax"):
        ids = lax.broadcasted_iota(jnp.int32, (1, piece), 1)
        hits = (ids + t * piece) == wanted[:, None]
        top = jnp.max(logits, axis=1)
        shifted = jnp.exp(logits - top[:, None])
        total = jnp.sum(shifted, axis=1)
        at_target = jnp.sum(jnp.where(hits, logits, 0.0), axis=1)
        shifted_low = jnp.where(hits, 0.0, shifted).astype(bf16)
        weighted = jnp.sum(shifted_low.astype(f32) * logits, axis=1)
        stats = jnp.stack([top, total, at_target, weighted])
    with jax.named_scope("grad_normed"):
        cross = flip(shifted_low, "tensor", n_tensor, 2)
        near = flip(shifted_low, "tensor", n_tensor, 1)
        there = swap(stats)
        products = [stream_rows(shifted_low, unembed_weight, t, 4)]
        cross, near, there, products = lax.optimization_barrier((cross, near, there, products))
        ends = lax.ppermute(cross, "tensor", [(2, 3), (1, 0)])
        middle = lax.ppermute(shifted_low, "tensor", [(1, 2), (2, 1)])
        pair_top = jnp.maximum(top, there[0])
        here_by, there_by = jnp.exp(top - pair_top), jnp.exp(there[0] - pair_top)
        stats = spread(
            jnp.stack(
                [
                    top,
                    pair_top,
                    total * here_by + there[1] * there_by,
                    at_target + there[2],
                    weighted * here_by + there[3] * there_by,
                ]
            )
        )
        products += [
            stream_rows(e, unembed_weight, t ^ r, 4) for r, e in ((1, near), (2, cross))
        ]
        ends, middle, stats, products = lax.optimization_barrier((ends, middle, stats, products))
        far = jnp.where((t == 0) | (t == n_tensor - 1), ends, middle)
        products.append(stream_rows(far, unembed_weight, t ^ 3, 4))
        shifted_parts = [shifted_low, near, cross, far]
        largest = jnp.max(jnp.stack([s[1] for s in stats]), axis=0)
        by = [jnp.exp(s[1] - largest) for s in stats]
        summed = sum(s[2] * b for s, b in zip(stats, by))
        hit_logit = sum(s[3] for s in stats)
        per_row = row_weights / summed
        hit_grad = row_weights * (jnp.exp(hit_logit - largest) / summed - 1.0)
        grad_dots = per_row * sum(s[4] * b for s, b in zip(stats, by)) + hit_grad * hit_logit
        factors = [per_row * jnp.exp(s[0] - largest) for s in stats]
        grad_part = hit_grad[:, None] * target_rows
        for factor, product in zip(factors, products):
            grad_part = grad_part + factor[:, None] * product
        grad_there = swap(grad_part.astype(bf16))
        grads = []
        for r, e in enumerate(shifted_parts):
            mine = (ids + (t ^ r) * piece) == wanted[:, None]
            grads.append(
                jnp.where(
                    mine, hit_grad[:, None], e.astype(f32) * factors[r][:, None]
                ).astype(bf16)
            )
        grad_stack = jnp.stack(grads)
        grad_slices = [
            lax.dynamic_index_in_dim(grad_stack, t ^ h ^ m, 0, keepdims=False)
            for m in range(n_head)
        ]
        grad_there, grad_slices = lax.optimization_barrier((grad_there, grad_slices))
    with jax.named_scope("grad_mixed"):
        grad_normed = grad_part + grad_there.astype(f32)
        grad_mixed = mixed_scale[:, None] * (
            grad_normed * final_gain[None, :] - mixed_normed * (grad_dots / features)[:, None]
        )
        grad_low = grad_mixed.astype(bf16)
        grad_scaled = (in_scale[:, None] * grad_mixed).astype(bf16)
        part_dots = jnp.sum(grad_low.astype(f32) * projected, axis=1)
        dots_high = lax.reduce_precision(part_dots, 8, 7)
        lane = lax.broadcasted_iota(jnp.int32, (1, 128), 1)
        extra = jnp.where(
            lane == 0,
            dots_high[:, None],
            jnp.where(lane == 1, (part_dots - dots_high)[:, None], 0.0),
        ).astype(bf16)
    with jax.named_scope("joined_grad"):
        sent = dot_columns_apart(grad_low, weight_block, [t ^ 3, t ^ 2, t ^ 1], width, extra)
        came = [flip(c, "tensor", n_tensor, r) for r, c in zip((3, 2, 1), sent)]
        heads_far = [flip(grad_slices[m], "head", n_head, m) for m in range(2, n_head)]
        side = dot_columns(grad_low, weight_block, t, width, 2, f32)
        order = t ^ jnp.arange(n_tensor, dtype=jnp.int32)
        combine_grad = combine_rows(jnp.stack(parts), grad_scaled, order, 2)[None]
        came, heads_far, side, combine_grad = lax.optimization_barrier(
            (came, heads_far, side, combine_grad)
        )
        for c in came:
            side = side + c[:, :width].astype(f32)
        dots = part_dots + sum(
            c[:, width].astype(f32) + c[:, width + 1].astype(f32) for c in came
        )
    with jax.named_scope("input_grads"):
        own_normed = own.astype(f32) * in_scale[:, None]
        term = in_scale[:, None] * (side - own_normed * (dots / features)[:, None])
        term = jnp.where(first, term + grad_mixed, term)
        term_low = term.astype(bf16)
        pair = flip(term_low, "head", n_head, 1)
        heads_near = flip(grad_slices[1], "head", n_head, 1)
        pair, heads_near = lax.optimization_barrier((pair, heads_near))
        pair = term_low.astype(f32) + pair.astype(f32)
        pair_low = pair.astype(bf16)
        crossed = swap(jnp.where(first, pair_low[half:], term_low[:half]))
        beside = lax.ppermute(
            pair_low[:half], ("head", "dp"), [(2 * i, 2 * (i ^ 2)) for i in range(n_head)]
        )
        across = lax.ppermute(
            pair_low[half:], ("head", "dp"), [(2 * i, 2 * (i ^ 2) + 1) for i in range(n_head)]
        )
        unembed_grad = head_sum([grad_slices[0], heads_near] + heads_far, normed_heads, 4)
        crossed, beside, across, unembed_grad = lax.optimization_barrier(
            (crossed, beside, across, unembed_grad)
        )
        unembed_grad = unembed_grad.reshape(1, 1, piece, width)
        embed_grad = jnp.where(first, crossed.astype(f32), term[half:])[None]
        trunk_grad = jnp.where(
            first,
            pair[:half] + beside.astype(f32),
            crossed.astype(f32) + across.astype(f32),
        )
    return (trunk_grad, embed_grad, combine_grad, unembed_grad)


def general_local(
    n_tensor,
    trunk_hidden,
    next_embeds,
    combine_weight,
    final_gain,
    unembed_weight,
    target_ids,
    loss_scale,
):
    rows, part_width = trunk_hidden.shape
    features = part_width * n_tensor
    vocab_part = unembed_weight.shape[0]
    weight_block = combine_weight[0]
    trunk_whole, embed_whole = (
        lax.all_gather(trunk_hidden, "tensor", axis=1, tiled=True),
        lax.all_gather(next_embeds[0], "tensor", axis=1, tiled=True),
    )
    trunk_float = trunk_whole.astype(f32)
    embed_float = embed_whole.astype(f32)
    trunk_scale = lax.rsqrt(jnp.sum(trunk_float * trunk_float, axis=1) / features + epsilon)
    embed_scale = lax.rsqrt(jnp.sum(embed_float * embed_float, axis=1) / features + epsilon)
    trunk_normed = trunk_float * trunk_scale[:, None]
    embed_normed = embed_float * embed_scale[:, None]
    joined = jnp.concatenate([trunk_normed.astype(bf16), embed_normed.astype(bf16)], axis=1)
    feature_start = lax.axis_index("tensor") * part_width
    trunk_local = lax.dynamic_slice_in_dim(trunk_normed, feature_start, part_width, 1)
    embed_local = lax.dynamic_slice_in_dim(embed_normed, feature_start, part_width, 1)
    blocks = lax.all_to_all(joined, "dp", split_axis=1, concat_axis=0, tiled=True)
    projected = lax.psum_scatter(
        plain_dot(blocks, weight_block).astype(bf16), "dp", scatter_dimension=0, tiled=True
    ).astype(f32)
    mixed = trunk_hidden.astype(f32) + projected
    mixed_sums = lax.psum(jnp.sum(mixed * mixed, axis=1), "tensor")
    mixed_scale = lax.rsqrt(mixed_sums / features + epsilon)
    mixed_normed = mixed * mixed_scale[:, None]
    normed_out = (mixed_normed * final_gain[None, :]).astype(bf16)
    normed_all = lax.all_gather(normed_out, "dp", axis=0, tiled=True)
    logits = lax.psum(contract_cols(normed_all, unembed_weight), "tensor")
    largest = lax.pmax(jnp.max(logits, axis=1), "dp")
    shifted = jnp.exp(logits - largest[:, None])
    summed = lax.psum(jnp.sum(shifted, axis=1), "dp")
    probs = shifted / summed[:, None]
    vocab_ids = (
        lax.broadcasted_iota(jnp.int32, (1, vocab_part), 1) + lax.axis_index("dp") * vocab_part
    )
    hits = (vocab_ids == target_ids[0][:, None]).astype(f32)
    grad_local = (loss_scale[0][:, None] * (probs - hits)).astype(bf16)
    grad_normed = lax.psum_scatter(
        plain_dot(grad_local, unembed_weight).astype(bf16), "dp", scatter_dimension=0, tiled=True
    ).astype(f32)
    vocab_term = contract_rows(grad_local, normed_all).astype(bf16)
    vocab_total = lax.psum_scatter(vocab_term, "head", scatter_dimension=0, tiled=True).astype(f32)
    unembed_grad = vocab_total.reshape(1, 1, vocab_total.shape[0], part_width)
    scaled_grad = grad_normed * final_gain[None, :]
    grad_dots = lax.psum(jnp.sum(scaled_grad * mixed_normed, axis=1), "tensor")
    grad_mixed = mixed_scale[:, None] * (
        scaled_grad - mixed_normed * (grad_dots / features)[:, None]
    )
    grad_all = lax.all_gather(grad_mixed.astype(bf16), "dp", axis=0, tiled=True)
    combine_grad = contract_rows(blocks, grad_all)[None]
    joined_part = lax.all_to_all(
        contract_cols(grad_all, weight_block).astype(bf16),
        "dp",
        split_axis=0,
        concat_axis=1,
        tiled=True,
    )
    joined_grad = lax.psum_scatter(
        joined_part.reshape(rows, 2, features), "tensor", scatter_dimension=2, tiled=True
    ).astype(f32)
    trunk_side = joined_grad[:, 0]
    embed_side = joined_grad[:, 1]
    trunk_dots, embed_dots = lax.psum(
        (jnp.sum(trunk_side * trunk_local, axis=1), jnp.sum(embed_side * embed_local, axis=1)),
        "tensor",
    )
    trunk_term = trunk_scale[:, None] * (
        trunk_side - trunk_local * (trunk_dots / features)[:, None]
    )
    embed_grad = (
        embed_scale[:, None] * (embed_side - embed_local * (embed_dots / features)[:, None])
    )[None]
    trunk_grad = lax.psum((grad_mixed + trunk_term).astype(bf16), "head").astype(f32)
    return (trunk_grad, embed_grad, combine_grad, unembed_grad)


def solution(mesh):
    n_head, n_tensor, n_dp = mesh.shape["head"], mesh.shape["tensor"], mesh.shape["dp"]
    in_specs = (
        P("dp", "tensor"),
        P("head", "dp", "tensor"),
        P("head", "dp", "tensor"),
        P("tensor"),
        P("dp", "tensor"),
        P("head", None),
        P("head", None),
    )
    out_specs = (
        P("dp", "tensor"),
        P("head", "dp", "tensor"),
        P("head", "dp", "tensor"),
        P("dp", "head", None, "tensor"),
    )
    if n_dp == 2 and n_tensor == 4 and n_head == 4:

        def local(*args):
            return fast_local(n_head, n_tensor, *args)

    else:

        def local(*args):
            return general_local(n_tensor, *args)

    return jax.shard_map(local, mesh=mesh, in_specs=in_specs, out_specs=out_specs, check_vma=False)
```

```python
import functools

import jax
import jax.numpy as jnp
from jax import lax
from jax.experimental import pallas as pl
from jax.experimental.pallas import tpu as pltpu
from jax.sharding import PartitionSpec as P

epsilon = 1e-05
f32 = jnp.float32
bf16 = jnp.bfloat16
kernel_memory = 16 << 20
brief = pl.CostEstimate(flops=0, bytes_accessed=0, transcendentals=0)
in_vmem = pl.BlockSpec(memory_space=pltpu.VMEM)
in_smem = pl.BlockSpec(memory_space=pltpu.SMEM)


def contract_rows(left, right):
    return lax.dot_general(
        left, right, (((0,), (0,)), ((), ())), preferred_element_type=f32
    )


def contract_cols(left, right):
    return lax.dot_general(
        left, right, (((1,), (1,)), ((), ())), preferred_element_type=f32
    )


def plain_dot(left, right):
    return jnp.dot(left, right, preferred_element_type=f32)


def flip(value, axis, size, mask):
    return lax.ppermute(value, axis, [(i, i ^ mask) for i in range(size)])


def swap(value):
    return lax.ppermute(value, "dp", [(0, 1), (1, 0)])


def params(memory):
    return pltpu.CompilerParams(vmem_limit_bytes=memory)


def shaped(*shape_and_type):
    *shape, dtype = shape_and_type
    return jax.ShapeDtypeStruct(tuple(shape), dtype)


def tensor_at(places):
    return places[0] % 16


def dp_at(places):
    return places[0] // 16


def whole_call(kernel, places, arrays, outs):
    return pl.pallas_call(
        kernel,
        out_shape=outs,
        in_specs=[in_smem] + [in_vmem] * len(arrays),
        out_specs=[in_vmem] * len(outs),
        compiler_params=params(kernel_memory),
        cost_estimate=brief,
    )(places, *arrays)


def join_rows(places, kept, given, put):
    half = kept.shape[0]

    @pl.when(dp_at(places) == 0)
    def _():
        put(slice(0, half), kept[...])
        put(slice(half, 2 * half), given[...])

    @pl.when(dp_at(places) != 0)
    def _():
        put(slice(0, half), given[...])
        put(slice(half, 2 * half), kept[...])


def column_block(j, block):
    return pl.ds(pl.multiple_of(j * block, 128), block)


def project_own_kernel(places, kept, given, weight, own, raw, squares):
    j = pl.program_id(0)

    @pl.when(j == 0)
    def _():
        def put(rows, value):
            own[rows] = value

        join_rows(places, kept, given, put)
        values = own[...].astype(f32)
        squares[...] = jnp.sum(values * values, axis=1, keepdims=True)
        raw[...] = jnp.zeros_like(raw)

    raw[...] += plain_dot(own[:, column_block(j, weight.shape[0])], weight[...])


def project_own(places, kept, given, weight, blocks):
    half, width = kept.shape
    rows = 2 * half
    fixed = lambda j, c: (0, 0)
    return pl.pallas_call(
        project_own_kernel,
        out_shape=[shaped(rows, width, bf16), shaped(rows, width, f32), shaped(rows, 1, f32)],
        grid_spec=pltpu.PrefetchScalarGridSpec(
            num_scalar_prefetch=1,
            grid=(blocks,),
            in_specs=[
                pl.BlockSpec((half, width), fixed),
                pl.BlockSpec((half, width), fixed),
                pl.BlockSpec((width // blocks, width), lambda j, c: (tensor_at(c) * blocks + j, 0)),
            ],
            out_specs=[
                pl.BlockSpec((rows, width), fixed),
                pl.BlockSpec((rows, width), fixed),
                pl.BlockSpec((rows, 1), fixed),
            ],
        ),
        compiler_params=params(kernel_memory),
        cost_estimate=brief,
    )(places, kept, given, weight)


def project_kernel(features, count, blocks, places, *refs):
    kept, given = refs[:count], refs[count : 2 * count]
    weight, raw, own_squares = refs[2 * count : 2 * count + 3]
    parts, projected, low, scale, held, done = refs[2 * count + 3 :]
    squares = own_squares[...]
    total = projected
    chunks = list(range(1, count + 1))
    for n, right in streamed(places, weight, chunks, blocks, held, done):
        k, j = n // blocks, n % blocks
        block = right.shape[0]
        if j == 0:

            def put(rows, value, k=k):
                parts[k, rows] = value

            join_rows(places, kept[k], given[k], put)
            values = parts[k].astype(f32)
            squares = squares + jnp.sum(values * values, axis=1, keepdims=True)
        product = plain_dot(parts[k, :, j * block : (j + 1) * block], right)
        total[...] = product + (raw[...] if n == 0 else total[...])
    scale[...] = lax.rsqrt(squares / features + epsilon)
    projected[...] = total[...] * scale[...]
    low[...] = projected[...].astype(bf16)


def project(places, kept, given, weight, raw, squares, features, blocks):
    count = len(kept)
    half, width = kept[0].shape
    rows = 2 * half
    return pl.pallas_call(
        functools.partial(project_kernel, features, count, blocks),
        out_shape=[
            shaped(count, rows, width, bf16),
            shaped(rows, width, f32),
            shaped(rows, width, bf16),
            shaped(rows, 1, f32),
        ],
        in_specs=[in_smem]
        + [in_vmem] * (2 * count)
        + [pl.BlockSpec(memory_space=pl.ANY), in_vmem, in_vmem],
        out_specs=[in_vmem] * 4,
        scratch_shapes=[
            pltpu.VMEM((count * blocks, width // blocks, width), weight.dtype),
            pltpu.SemaphoreType.DMA((count * blocks,)),
        ],
        compiler_params=params(kernel_memory),
        cost_estimate=brief,
    )(places, *kept, *given, weight, raw, squares)


def held_columns_kernel(count, _, left, *refs):
    rights, extras, outs = refs[:count], refs[count:-count], refs[-count:]
    size = rights[0].shape[0]
    for right, out in zip(rights, outs):
        out[:, :size] = contract_cols(left[...], right[...]).astype(out.dtype)
        for extra in extras:
            out[:, size:] = extra[...]


def held_columns(places, left, rights, dtype, extra=None):
    extras = [] if extra is None else [extra]
    wide = rights[0].shape[0] + sum(e.shape[1] for e in extras)
    return whole_call(
        functools.partial(held_columns_kernel, len(rights)),
        places,
        [left] + rights + extras,
        [shaped(left.shape[0], wide, dtype) for _ in rights],
    )


def held_between_kernel(places, outer, inner, right, out):
    t = tensor_at(places)
    left = jnp.where((t == 0) | (t == 3), outer[...], inner[...])
    out[...] = plain_dot(left, right[...])


def streamed(places, weight, chunks, blocks, held, done):
    slots, block, _ = held.shape
    copies = []
    for n in range(blocks * len(chunks)):
        start = (n % blocks) * block
        if chunks[n // blocks] is not None:
            place = tensor_at(places) ^ chunks[n // blocks]
            start = pl.multiple_of(place * (blocks * block) + start, block)
        slot = n % slots
        copies.append(
            pltpu.make_async_copy(weight.at[pl.ds(start, block)], held.at[slot], done.at[slot])
        )
    for copy in copies[:slots]:
        copy.start()
    for n, copy in enumerate(copies):
        copy.wait()
        yield n, held[n % slots]
        if n + slots < len(copies):
            copies[n + slots].start()


def stream_columns_kernel(chunks, blocks, places, left, weight, *refs):
    outs, (held, done) = refs[:-2], refs[-2:]
    block = held.shape[1]
    for n, right in streamed(places, weight, chunks, blocks, held, done):
        j = n % blocks
        product = contract_cols(left[...], right)
        outs[n // blocks][:, j * block : (j + 1) * block] = product.astype(outs[0].dtype)


def stream_rows_kernel(chunks, blocks, places, *refs):
    count = len(chunks)
    lefts, weight, outs, (held, done) = refs[:count], refs[count], refs[count + 1 : -2], refs[-2:]
    block = held.shape[1]
    for n, right in streamed(places, weight, chunks, blocks, held, done):
        k, j = n // blocks, n % blocks
        product = plain_dot(lefts[k][:, j * block : (j + 1) * block], right)
        if j == 0:
            outs[k][...] = product
        else:
            outs[k][...] += product


def stream(kernel, places, lefts, weight, chunks, size, outs, blocks, slots):
    return pl.pallas_call(
        functools.partial(kernel, chunks, blocks),
        out_shape=outs,
        in_specs=[in_smem] + [in_vmem] * len(lefts) + [pl.BlockSpec(memory_space=pl.ANY)],
        out_specs=[in_vmem] * len(outs),
        scratch_shapes=[
            pltpu.VMEM((slots, size // blocks, weight.shape[1]), weight.dtype),
            pltpu.SemaphoreType.DMA((slots,)),
        ],
        compiler_params=params(kernel_memory),
        cost_estimate=brief,
    )(places, *lefts, weight)


def stream_columns(places, left, weight, chunks, size, blocks, dtype):
    outs = [shaped(left.shape[0], size, dtype) for _ in chunks]
    slots = blocks * len(chunks)
    return stream(
        stream_columns_kernel, places, [left], weight, chunks, size, outs, blocks, slots
    )


def stream_rows(places, lefts, weight, chunks, blocks, slots):
    rows, size = lefts[0].shape
    outs = [shaped(rows, weight.shape[1], f32) for _ in chunks]
    return stream(
        stream_rows_kernel, places, lefts, weight, chunks, size, outs, blocks, slots
    )


def combine_kernel(places, own, part, grad, out):
    c = pl.program_id(0)

    @pl.when(tensor_at(places) == c)
    def _():
        out[...] = contract_rows(own[...], grad[...])

    @pl.when(tensor_at(places) != c)
    def _():
        out[...] = contract_rows(part[0], grad[...])


def combine(places, own, parts, grad):
    rows, width = own.shape
    count = parts.shape[0] + 1
    fixed = lambda c, w: (0, 0)
    return pl.pallas_call(
        combine_kernel,
        out_shape=shaped(count * width, grad.shape[1], f32),
        grid_spec=pltpu.PrefetchScalarGridSpec(
            num_scalar_prefetch=1,
            grid=(count,),
            in_specs=[
                pl.BlockSpec((rows, width), fixed),
                pl.BlockSpec(
                    (1, rows, width), lambda c, w: (jnp.maximum((tensor_at(w) ^ c) - 1, 0), 0, 0)
                ),
                pl.BlockSpec((rows, grad.shape[1]), fixed),
            ],
            out_specs=pl.BlockSpec((width, grad.shape[1]), lambda c, w: (c, 0)),
        ),
        compiler_params=params(kernel_memory),
        cost_estimate=brief,
    )(places, own, parts, grad)


def head_sum_kernel(*refs):
    out = refs[-1]
    count = (len(refs) - 1) // 2
    left = jnp.concatenate([r[...] for r in refs[:count]], axis=0)
    right = jnp.concatenate([r[...] for r in refs[count : 2 * count]], axis=0)
    out[...] = contract_rows(left, right)


def head_sum(grads, normed, blocks):
    rows, size = grads[0].shape
    width = normed[0].shape[1]
    block = size // blocks
    return pl.pallas_call(
        head_sum_kernel,
        out_shape=shaped(size, width, f32),
        grid=(blocks,),
        in_specs=[pl.BlockSpec((rows, block), lambda j: (0, j))] * len(grads)
        + [pl.BlockSpec((rows, width), lambda j: (0, 0))] * len(normed),
        out_specs=pl.BlockSpec((block, width), lambda j: (j, 0)),
        compiler_params=params(kernel_memory),
        cost_estimate=brief,
    )(*grads, *normed)


def input_grad_kernel(features, places, side, own, in_scale, grad_mixed, dots, *refs):
    came, (term, term_low) = refs[:-2], refs[-2:]
    width = side.shape[1]
    total = side[...]
    dot = dots[...]
    for each in came:
        total = total + each[:, :width].astype(f32)
        dot = dot + (
            each[:, width : width + 1].astype(f32) + each[:, width + 1 : width + 2].astype(f32)
        )
    normed = own[...].astype(f32) * in_scale[...]
    value = in_scale[...] * (total - normed * (dot / features))
    value = value + jnp.where(dp_at(places) == 0, grad_mixed[...], 0.0)
    term[...] = value
    term_low[...] = value.astype(bf16)


def fast_local(
    n_head,
    n_tensor,
    trunk_hidden,
    next_embeds,
    combine_weight,
    final_gain,
    unembed_weight,
    target_ids,
    loss_scale,
):
    half, width = trunk_hidden.shape
    rows = 2 * half
    features = width * n_tensor
    vocab_part = unembed_weight.shape[0]
    piece = vocab_part // n_tensor
    combine_whole, unembed_whole = combine_weight[0], unembed_weight
    weight_block = pltpu.with_memory_space_constraint(combine_weight[0], pltpu.HBM)
    unembed_weight = pltpu.with_memory_space_constraint(unembed_weight, pltpu.HBM)
    d = lax.axis_index("dp")
    t = lax.axis_index("tensor")
    h = lax.axis_index("head")
    first = d == 0
    places = (t + 16 * d).astype(jnp.int32).reshape(1)
    row_weights = loss_scale[0]

    def chunk_of(weight, r, size):
        return lax.dynamic_slice_in_dim(weight, (t ^ r) * size, size, 0)

    def spread(value):
        return [value] + [flip(value, "tensor", n_tensor, r) for r in range(1, n_tensor)]

    with jax.named_scope("inputs"):
        embeds = next_embeds[0]
        kept = jnp.where(first, trunk_hidden, embeds)
        given = jnp.where(first, embeds, trunk_hidden)
        kept_parts = spread(kept)
        swapped = swap(given)
        kept_parts, swapped = lax.optimization_barrier((kept_parts, swapped))
        given_parts = spread(swapped)
        trunk_other = swap(trunk_hidden)
        own, raw, squares = project_own(places, kept_parts[0], swapped, weight_block, 2)
        given_parts, trunk_other, own, raw, squares = lax.optimization_barrier(
            (given_parts, trunk_other, own, raw, squares)
        )
    with jax.named_scope("projection"):
        parts, projected, projected_low, in_scale = project(
            places, kept_parts[1:], given_parts[1:], weight_block, raw, squares, features, 2
        )
        projected_there = swap(projected_low)
        weight_far = chunk_of(unembed_whole, 3, piece)
        projected_there, weight_far = lax.optimization_barrier((projected_there, weight_far))
        trunk_rows = jnp.where(
            first, own, jnp.concatenate([trunk_other, trunk_hidden], axis=0)
        ).astype(f32)
        mixed = trunk_rows + (projected + projected_there.astype(f32))
        gained = mixed * final_gain[None, :]
        low = gained.astype(bf16)
    with jax.named_scope("logits"):
        (far,) = held_columns(places, low, [weight_far], f32)
        ends = lax.ppermute(far, "tensor", [(0, 1), (3, 2)])
        middle = lax.ppermute(far, "tensor", [(1, 2), (2, 1)])
        mixed_squares = spread(jnp.sum(mixed * mixed, axis=1))
        cross, near = stream_columns(places, low, unembed_weight, [2, 1], piece, 4, f32)
        wanted = (target_ids[0] - d * vocab_part)[:, None]
        ends, middle, mixed_squares, cross, near, low, wanted = lax.optimization_barrier(
            (ends, middle, mixed_squares, cross, near, low, wanted)
        )
        mixed_scale = lax.rsqrt(sum(mixed_squares) / features + epsilon)[:, None]
        normed_out = (gained * mixed_scale).astype(bf16)
        normed_heads = [normed_out] + [
            flip(normed_out, "head", n_head, m) for m in range(1, n_head)
        ]
        cross = flip(cross + ends, "tensor", n_tensor, 2)
        near = flip(near, "tensor", n_tensor, 1)
        chosen = lax.broadcasted_iota(jnp.int32, (1, vocab_part), 1) == wanted
        (target_rows,) = stream_rows(
            places, [chosen.astype(bf16)], unembed_weight, [None], 16, 8
        )
        (last,) = stream_columns(places, low, unembed_weight, [0], piece, 4, f32)
        cross, near, normed_heads, target_rows, last = lax.optimization_barrier(
            (cross, near, normed_heads, target_rows, last)
        )
        logits = (last + middle + cross + near) * mixed_scale
    with jax.named_scope("softmax"):
        hits = (lax.broadcasted_iota(jnp.int32, (1, piece), 1) + t * piece) == wanted
        top = jnp.max(logits, axis=1)
        shifted = jnp.exp(logits - top[:, None])
        shifted_low = jnp.where(hits, 0.0, shifted).astype(bf16)
        stats = jnp.stack(
            [
                top,
                jnp.sum(shifted, axis=1),
                jnp.sum(jnp.where(hits, logits, 0.0), axis=1),
                jnp.sum(shifted_low.astype(f32) * logits, axis=1),
            ]
        )
    with jax.named_scope("grad_normed"):
        cross = flip(shifted_low, "tensor", n_tensor, 2)
        near = flip(shifted_low, "tensor", n_tensor, 1)
        there = swap(stats)
        products = stream_rows(places, [shifted_low], unembed_weight, [0], 4, 4)
        weight_sent = [chunk_of(combine_whole, r, width) for r in (3, 2, 1)]
        weight_far = chunk_of(unembed_whole, 3, piece)
        cross, near, there, products, value, weight_sent, weight_far = lax.optimization_barrier(
            (cross, near, there, products, shifted_low, weight_sent, weight_far)
        )
        ends = lax.ppermute(cross, "tensor", [(2, 3), (1, 0)])
        middle = lax.ppermute(value, "tensor", [(1, 2), (2, 1)])
        pair_top = jnp.maximum(top, there[0])
        here_by, there_by = jnp.exp(top - pair_top), jnp.exp(there[0] - pair_top)
        stats = spread(
            jnp.stack(
                [
                    top,
                    pair_top,
                    stats[1] * here_by + there[1] * there_by,
                    stats[2] + there[2],
                    stats[3] * here_by + there[3] * there_by,
                ]
            )
        )
        stats, near, cross = lax.optimization_barrier((stats, near, cross))
        products += stream_rows(places, [near, cross], unembed_weight, [1, 2], 4, 8)
        ends, middle, products = lax.optimization_barrier((ends, middle, products))
        products += whole_call(
            held_between_kernel,
            places,
            [ends, middle, weight_far],
            [shaped(rows, width, f32)],
        )
        far = jnp.where((t == 0) | (t == n_tensor - 1), ends, middle)
        shifted_parts = [shifted_low, near, cross, far]
        largest = jnp.max(jnp.stack([s[1] for s in stats]), axis=0)
        by = [jnp.exp(s[1] - largest) for s in stats]
        summed = sum(s[2] * b for s, b in zip(stats, by))
        hit_logit = sum(s[3] for s in stats)
        per_row = row_weights / summed
        hit_grad = row_weights * (jnp.exp(hit_logit - largest) / summed - 1.0)
        grad_dots = per_row * sum(s[4] * b for s, b in zip(stats, by)) + hit_grad * hit_logit
        factors = [per_row * jnp.exp(s[0] - largest) for s in stats]
        grad_part = hit_grad[:, None] * target_rows
        for r, product in enumerate(products):
            grad_part = grad_part + factors[r][:, None] * product
        grad_there = swap(grad_part.astype(bf16))
        ids = lax.broadcasted_iota(jnp.int32, (1, piece), 1)
        grad_stack = jnp.stack(
            [
                jnp.where(
                    (ids + (t ^ r) * piece) == wanted,
                    hit_grad[:, None],
                    e.astype(f32) * factors[r][:, None],
                ).astype(bf16)
                for r, e in enumerate(shifted_parts)
            ]
        )
        grad_slices = [
            lax.dynamic_index_in_dim(grad_stack, t ^ h ^ m, 0, keepdims=False)
            for m in range(n_head)
        ]
        grad_there, grad_slices = lax.optimization_barrier((grad_there, grad_slices))
    with jax.named_scope("grad_mixed"):
        grad_normed = grad_part + grad_there.astype(f32)
        mixed_normed = mixed * mixed_scale
        grad_mixed = mixed_scale * (
            grad_normed * final_gain[None, :] - mixed_normed * (grad_dots / features)[:, None]
        )
        grad_low = grad_mixed.astype(bf16)
        grad_scaled = (in_scale * grad_mixed).astype(bf16)
        dots = jnp.sum(grad_low.astype(f32) * projected, axis=1, keepdims=True)
        dots_high = lax.reduce_precision(dots, 8, 7)
        lane = lax.broadcasted_iota(jnp.int32, (1, 128), 1)
        extra = jnp.where(
            lane == 0, dots_high, jnp.where(lane == 1, dots - dots_high, 0.0)
        ).astype(bf16)
    with jax.named_scope("joined_grad"):
        sent = held_columns(places, grad_low, weight_sent, bf16, extra)
        came = [flip(c, "tensor", n_tensor, r) for r, c in zip((3, 2, 1), sent)]
        heads_given = [flip(grad_slices[m], "head", n_head, m) for m in range(1, n_head)]
        (side,) = stream_columns(places, grad_low, weight_block, [0], width, 2, f32)
        combine_grad = combine(places, own, parts, grad_scaled)[None]
        unembed_grad = head_sum([grad_slices[0]] + heads_given, normed_heads, 2)
        unembed_grad = unembed_grad.reshape(1, 1, piece, width)
        came, side, combine_grad, unembed_grad = lax.optimization_barrier(
            (came, side, combine_grad, unembed_grad)
        )
    with jax.named_scope("input_grads"):
        term, term_low = whole_call(
            functools.partial(input_grad_kernel, features),
            places,
            [side, own, in_scale, grad_mixed, dots] + came,
            [shaped(rows, width, f32), shaped(rows, width, bf16)],
        )
        pair = flip(term_low, "head", n_head, 1)
        pair = term_low.astype(f32) + pair.astype(f32)
        pair_low = pair.astype(bf16)
        crossed = swap(jnp.where(first, pair_low[half:], term_low[:half]))
        beside = lax.ppermute(
            pair_low[:half], ("head", "dp"), [(2 * i, 2 * (i ^ 2)) for i in range(n_head)]
        )
        across = lax.ppermute(
            pair_low[half:], ("head", "dp"), [(2 * i, 2 * (i ^ 2) + 1) for i in range(n_head)]
        )
        crossed, beside, across = [v.astype(f32) for v in (crossed, beside, across)]
        embed_grad = jnp.where(first, crossed, term[half:])[None]
        trunk_grad = jnp.where(first, pair[:half] + beside, crossed + across)
    return (trunk_grad, embed_grad, combine_grad, unembed_grad)


def general_local(
    n_tensor,
    trunk_hidden,
    next_embeds,
    combine_weight,
    final_gain,
    unembed_weight,
    target_ids,
    loss_scale,
):
    rows, part_width = trunk_hidden.shape
    features = part_width * n_tensor
    vocab_part = unembed_weight.shape[0]
    weight_block = combine_weight[0]
    trunk_whole, embed_whole = (
        lax.all_gather(trunk_hidden, "tensor", axis=1, tiled=True),
        lax.all_gather(next_embeds[0], "tensor", axis=1, tiled=True),
    )
    trunk_float = trunk_whole.astype(f32)
    embed_float = embed_whole.astype(f32)
    trunk_scale = lax.rsqrt(jnp.sum(trunk_float * trunk_float, axis=1) / features + epsilon)
    embed_scale = lax.rsqrt(jnp.sum(embed_float * embed_float, axis=1) / features + epsilon)
    trunk_normed = trunk_float * trunk_scale[:, None]
    embed_normed = embed_float * embed_scale[:, None]
    joined = jnp.concatenate([trunk_normed.astype(bf16), embed_normed.astype(bf16)], axis=1)
    feature_start = lax.axis_index("tensor") * part_width
    trunk_local = lax.dynamic_slice_in_dim(trunk_normed, feature_start, part_width, 1)
    embed_local = lax.dynamic_slice_in_dim(embed_normed, feature_start, part_width, 1)
    blocks = lax.all_to_all(joined, "dp", split_axis=1, concat_axis=0, tiled=True)
    projected = lax.psum_scatter(
        plain_dot(blocks, weight_block).astype(bf16), "dp", scatter_dimension=0, tiled=True
    ).astype(f32)
    mixed = trunk_hidden.astype(f32) + projected
    mixed_sums = lax.psum(jnp.sum(mixed * mixed, axis=1), "tensor")
    mixed_scale = lax.rsqrt(mixed_sums / features + epsilon)
    mixed_normed = mixed * mixed_scale[:, None]
    normed_out = (mixed_normed * final_gain[None, :]).astype(bf16)
    normed_all = lax.all_gather(normed_out, "dp", axis=0, tiled=True)
    logits = lax.psum(contract_cols(normed_all, unembed_weight), "tensor")
    largest = lax.pmax(jnp.max(logits, axis=1), "dp")
    shifted = jnp.exp(logits - largest[:, None])
    summed = lax.psum(jnp.sum(shifted, axis=1), "dp")
    probs = shifted / summed[:, None]
    vocab_ids = (
        lax.broadcasted_iota(jnp.int32, (1, vocab_part), 1) + lax.axis_index("dp") * vocab_part
    )
    hits = (vocab_ids == target_ids[0][:, None]).astype(f32)
    grad_local = (loss_scale[0][:, None] * (probs - hits)).astype(bf16)
    grad_normed = lax.psum_scatter(
        plain_dot(grad_local, unembed_weight).astype(bf16), "dp", scatter_dimension=0, tiled=True
    ).astype(f32)
    vocab_term = contract_rows(grad_local, normed_all).astype(bf16)
    vocab_total = lax.psum_scatter(vocab_term, "head", scatter_dimension=0, tiled=True).astype(f32)
    unembed_grad = vocab_total.reshape(1, 1, vocab_total.shape[0], part_width)
    scaled_grad = grad_normed * final_gain[None, :]
    grad_dots = lax.psum(jnp.sum(scaled_grad * mixed_normed, axis=1), "tensor")
    grad_mixed = mixed_scale[:, None] * (
        scaled_grad - mixed_normed * (grad_dots / features)[:, None]
    )
    grad_all = lax.all_gather(grad_mixed.astype(bf16), "dp", axis=0, tiled=True)
    combine_grad = contract_rows(blocks, grad_all)[None]
    joined_part = lax.all_to_all(
        contract_cols(grad_all, weight_block).astype(bf16),
        "dp",
        split_axis=0,
        concat_axis=1,
        tiled=True,
    )
    joined_grad = lax.psum_scatter(
        joined_part.reshape(rows, 2, features), "tensor", scatter_dimension=2, tiled=True
    ).astype(f32)
    trunk_side = joined_grad[:, 0]
    embed_side = joined_grad[:, 1]
    trunk_dots, embed_dots = lax.psum(
        (jnp.sum(trunk_side * trunk_local, axis=1), jnp.sum(embed_side * embed_local, axis=1)),
        "tensor",
    )
    trunk_term = trunk_scale[:, None] * (
        trunk_side - trunk_local * (trunk_dots / features)[:, None]
    )
    embed_grad = (
        embed_scale[:, None] * (embed_side - embed_local * (embed_dots / features)[:, None])
    )[None]
    trunk_grad = lax.psum((grad_mixed + trunk_term).astype(bf16), "head").astype(f32)
    return (trunk_grad, embed_grad, combine_grad, unembed_grad)


def solution(mesh):
    n_head, n_tensor, n_dp = mesh.shape["head"], mesh.shape["tensor"], mesh.shape["dp"]
    in_specs = (
        P("dp", "tensor"),
        P("head", "dp", "tensor"),
        P("head", "dp", "tensor"),
        P("tensor"),
        P("dp", "tensor"),
        P("head", None),
        P("head", None),
    )
    out_specs = (
        P("dp", "tensor"),
        P("head", "dp", "tensor"),
        P("head", "dp", "tensor"),
        P("dp", "head", None, "tensor"),
    )
    if n_dp == 2 and n_tensor == 4 and n_head == 4:

        def local(*args):
            return fast_local(n_head, n_tensor, *args)

    else:

        def local(*args):
            return general_local(n_tensor, *args)

    return jax.shard_map(local, mesh=mesh, in_specs=in_specs, out_specs=out_specs, check_vma=False)
```

```python
import functools

import jax
import jax.numpy as jnp
from jax import lax
from jax.experimental import pallas as pl
from jax.experimental.pallas import tpu as pltpu
from jax.sharding import PartitionSpec as P

epsilon = 1e-05
f32 = jnp.float32
bf16 = jnp.bfloat16
kernel_memory = 16 << 20
brief = pl.CostEstimate(flops=0, bytes_accessed=0, transcendentals=0)
in_vmem = pl.BlockSpec(memory_space=pltpu.VMEM)
in_smem = pl.BlockSpec(memory_space=pltpu.SMEM)


def contract_rows(left, right):
    return lax.dot_general(
        left, right, (((0,), (0,)), ((), ())), preferred_element_type=f32
    )


def contract_cols(left, right):
    return lax.dot_general(
        left, right, (((1,), (1,)), ((), ())), preferred_element_type=f32
    )


def plain_dot(left, right):
    return jnp.dot(left, right, preferred_element_type=f32)


def flip(value, axis, size, mask):
    return lax.ppermute(value, axis, [(i, i ^ mask) for i in range(size)])


def swap(value):
    return lax.ppermute(value, "dp", [(0, 1), (1, 0)])


def params(memory):
    return pltpu.CompilerParams(vmem_limit_bytes=memory)


def shaped(*shape_and_type):
    *shape, dtype = shape_and_type
    return jax.ShapeDtypeStruct(tuple(shape), dtype)


def tensor_at(places):
    return places[0] % 16


def dp_at(places):
    return places[0] // 16


def whole_call(kernel, places, arrays, outs):
    return pl.pallas_call(
        kernel,
        out_shape=outs,
        in_specs=[in_smem] + [in_vmem] * len(arrays),
        out_specs=[in_vmem] * len(outs),
        compiler_params=params(kernel_memory),
        cost_estimate=brief,
    )(places, *arrays)


def join_rows(places, kept, given, put):
    half = kept.shape[0]

    @pl.when(dp_at(places) == 0)
    def _():
        put(slice(0, half), kept[...])
        put(slice(half, 2 * half), given[...])

    @pl.when(dp_at(places) != 0)
    def _():
        put(slice(0, half), given[...])
        put(slice(half, 2 * half), kept[...])


def column_block(j, block):
    return pl.ds(pl.multiple_of(j * block, 128), block)


def project_own_kernel(places, kept, given, weight, own, raw, squares):
    j = pl.program_id(0)

    @pl.when(j == 0)
    def _():
        def put(rows, value):
            own[rows] = value

        join_rows(places, kept, given, put)
        values = own[...].astype(f32)
        squares[...] = jnp.sum(values * values, axis=1, keepdims=True)
        raw[...] = jnp.zeros_like(raw)

    raw[...] += plain_dot(own[:, column_block(j, weight.shape[0])], weight[...])


def project_own(places, kept, given, weight, blocks):
    half, width = kept.shape
    rows = 2 * half
    fixed = lambda j, c: (0, 0)
    return pl.pallas_call(
        project_own_kernel,
        out_shape=[shaped(rows, width, bf16), shaped(rows, width, f32), shaped(rows, 1, f32)],
        grid_spec=pltpu.PrefetchScalarGridSpec(
            num_scalar_prefetch=1,
            grid=(blocks,),
            in_specs=[
                pl.BlockSpec((half, width), fixed),
                pl.BlockSpec((half, width), fixed),
                pl.BlockSpec((width // blocks, width), lambda j, c: (tensor_at(c) * blocks + j, 0)),
            ],
            out_specs=[
                pl.BlockSpec((rows, width), fixed),
                pl.BlockSpec((rows, width), fixed),
                pl.BlockSpec((rows, 1), fixed),
            ],
        ),
        compiler_params=params(kernel_memory),
        cost_estimate=brief,
    )(places, kept, given, weight)


def project_kernel(features, count, blocks, places, *refs):
    kept, given = refs[:count], refs[count : 2 * count]
    weight, raw, own_squares = refs[2 * count : 2 * count + 3]
    parts_out, projected, low, scale, parts, held, done, written = refs[2 * count + 3 :]
    writes = [
        pltpu.make_async_copy(parts.at[k], parts_out.at[k], written.at[k]) for k in range(count)
    ]
    squares = own_squares[...]
    total = projected
    chunks = list(range(1, count + 1))
    for n, right in streamed(places, weight, chunks, blocks, held, done):
        k, j = n // blocks, n % blocks
        block = right.shape[0]
        if j == 0:

            def put(rows, value, k=k):
                parts[k, rows] = value

            join_rows(places, kept[k], given[k], put)
            writes[k].start()
            values = parts[k].astype(f32)
            squares = squares + jnp.sum(values * values, axis=1, keepdims=True)
        product = plain_dot(parts[k, :, j * block : (j + 1) * block], right)
        total[...] = product + (raw[...] if n == 0 else total[...])
    scale[...] = lax.rsqrt(squares / features + epsilon)
    projected[...] = total[...] * scale[...]
    low[...] = projected[...].astype(bf16)
    for write in writes:
        write.wait()


def project(places, kept, given, weight, raw, squares, features, blocks):
    count = len(kept)
    half, width = kept[0].shape
    rows = 2 * half
    return pl.pallas_call(
        functools.partial(project_kernel, features, count, blocks),
        out_shape=[
            pltpu.HBM((count, rows, width), bf16),
            shaped(rows, width, f32),
            shaped(rows, width, bf16),
            shaped(rows, 1, f32),
        ],
        in_specs=[in_smem]
        + [in_vmem] * (2 * count)
        + [pl.BlockSpec(memory_space=pl.ANY), in_vmem, in_vmem],
        out_specs=[pl.BlockSpec(memory_space=pl.ANY)] + [in_vmem] * 3,
        scratch_shapes=[
            pltpu.VMEM((count, rows, width), bf16),
            pltpu.VMEM((count * blocks, width // blocks, width), weight.dtype),
            pltpu.SemaphoreType.DMA((count * blocks,)),
            pltpu.SemaphoreType.DMA((count,)),
        ],
        compiler_params=params(kernel_memory),
        cost_estimate=brief,
    )(places, *kept, *given, weight, raw, squares)


def held_columns_kernel(count, _, left, *refs):
    rights, extras, outs = refs[:count], refs[count:-count], refs[-count:]
    size = rights[0].shape[0]
    for right, out in zip(rights, outs):
        out[:, :size] = contract_cols(left[...], right[...]).astype(out.dtype)
        for extra in extras:
            out[:, size:] = extra[...]


def held_columns(places, left, rights, dtype, extra=None):
    extras = [] if extra is None else [extra]
    wide = rights[0].shape[0] + sum(e.shape[1] for e in extras)
    return whole_call(
        functools.partial(held_columns_kernel, len(rights)),
        places,
        [left] + rights + extras,
        [shaped(left.shape[0], wide, dtype) for _ in rights],
    )


def held_between_kernel(places, outer, inner, right, out):
    t = tensor_at(places)
    left = jnp.where((t == 0) | (t == 3), outer[...], inner[...])
    out[...] = plain_dot(left, right[...])


def streamed(places, weight, chunks, blocks, held, done):
    slots, block, _ = held.shape
    copies = []
    for n in range(blocks * len(chunks)):
        start = (n % blocks) * block
        if chunks[n // blocks] is not None:
            place = tensor_at(places) ^ chunks[n // blocks]
            start = pl.multiple_of(place * (blocks * block) + start, block)
        slot = n % slots
        copies.append(
            pltpu.make_async_copy(weight.at[pl.ds(start, block)], held.at[slot], done.at[slot])
        )
    for copy in copies[:slots]:
        copy.start()
    for n, copy in enumerate(copies):
        copy.wait()
        yield n, held[n % slots]
        if n + slots < len(copies):
            copies[n + slots].start()


def stream_columns_kernel(chunks, blocks, places, left, weight, *refs):
    outs, (held, done) = refs[:-2], refs[-2:]
    block = held.shape[1]
    for n, right in streamed(places, weight, chunks, blocks, held, done):
        j = n % blocks
        product = contract_cols(left[...], right)
        outs[n // blocks][:, j * block : (j + 1) * block] = product.astype(outs[0].dtype)


def stream_rows_kernel(chunks, blocks, places, *refs):
    count = len(chunks)
    lefts, weight, outs, (held, done) = refs[:count], refs[count], refs[count + 1 : -2], refs[-2:]
    block = held.shape[1]
    for n, right in streamed(places, weight, chunks, blocks, held, done):
        k, j = n // blocks, n % blocks
        product = plain_dot(lefts[k][:, j * block : (j + 1) * block], right)
        if j == 0:
            outs[k][...] = product
        else:
            outs[k][...] += product


def stream(kernel, places, lefts, weight, chunks, size, outs, blocks, slots):
    return pl.pallas_call(
        functools.partial(kernel, chunks, blocks),
        out_shape=outs,
        in_specs=[in_smem] + [in_vmem] * len(lefts) + [pl.BlockSpec(memory_space=pl.ANY)],
        out_specs=[in_vmem] * len(outs),
        scratch_shapes=[
            pltpu.VMEM((slots, size // blocks, weight.shape[1]), weight.dtype),
            pltpu.SemaphoreType.DMA((slots,)),
        ],
        compiler_params=params(kernel_memory),
        cost_estimate=brief,
    )(places, *lefts, weight)


def stream_columns(places, left, weight, chunks, size, blocks, dtype):
    outs = [shaped(left.shape[0], size, dtype) for _ in chunks]
    slots = blocks * len(chunks)
    return stream(
        stream_columns_kernel, places, [left], weight, chunks, size, outs, blocks, slots
    )


def stream_rows(places, lefts, weight, chunks, blocks, slots):
    rows, size = lefts[0].shape
    outs = [shaped(rows, weight.shape[1], f32) for _ in chunks]
    return stream(
        stream_rows_kernel, places, lefts, weight, chunks, size, outs, blocks, slots
    )


def combine_kernel(places, own, part, grad, out):
    c = pl.program_id(0)

    @pl.when(tensor_at(places) == c)
    def _():
        out[...] = contract_rows(own[...], grad[...])

    @pl.when(tensor_at(places) != c)
    def _():
        out[...] = contract_rows(part[0], grad[...])


def combine(places, own, parts, grad):
    rows, width = own.shape
    count = parts.shape[0] + 1
    fixed = lambda c, w: (0, 0)
    return pl.pallas_call(
        combine_kernel,
        out_shape=shaped(count * width, grad.shape[1], f32),
        grid_spec=pltpu.PrefetchScalarGridSpec(
            num_scalar_prefetch=1,
            grid=(count,),
            in_specs=[
                pl.BlockSpec((rows, width), fixed),
                pl.BlockSpec(
                    (1, rows, width), lambda c, w: (jnp.maximum((tensor_at(w) ^ c) - 1, 0), 0, 0)
                ),
                pl.BlockSpec((rows, grad.shape[1]), fixed),
            ],
            out_specs=pl.BlockSpec((width, grad.shape[1]), lambda c, w: (c, 0)),
        ),
        compiler_params=params(kernel_memory),
        cost_estimate=brief,
    )(places, own, parts, grad)


def head_sum_kernel(*refs):
    out = refs[-1]
    count = (len(refs) - 1) // 2
    left = jnp.concatenate([r[...] for r in refs[:count]], axis=0)
    right = jnp.concatenate([r[...] for r in refs[count : 2 * count]], axis=0)
    out[...] = contract_rows(left, right)


def head_sum(grads, normed, blocks):
    rows, size = grads[0].shape
    width = normed[0].shape[1]
    block = size // blocks
    return pl.pallas_call(
        head_sum_kernel,
        out_shape=shaped(size, width, f32),
        grid=(blocks,),
        in_specs=[pl.BlockSpec((rows, block), lambda j: (0, j))] * len(grads)
        + [pl.BlockSpec((rows, width), lambda j: (0, 0))] * len(normed),
        out_specs=pl.BlockSpec((block, width), lambda j: (j, 0)),
        compiler_params=params(kernel_memory),
        cost_estimate=brief,
    )(*grads, *normed)


def softmax_factors_kernel(_, here, there, weights, scale, out):
    count = here.shape[0]
    shards = [[r[n, k : k + 1, :] for k in range(4)] for r in (here, there) for n in range(count)]
    largest = shards[0][0]
    for shard in shards[1:]:
        largest = jnp.maximum(largest, shard[0])
    by = [jnp.exp(shard[0] - largest) for shard in shards]
    summed = sum(shard[1] * b for shard, b in zip(shards, by))
    hit_logit = sum(shard[2] for shard in shards)
    weighted = sum(shard[3] * b for shard, b in zip(shards, by))
    per_row = weights[...] / summed
    hit_grad = weights[...] * (jnp.exp(hit_logit - largest) / summed - 1.0)
    out[0:1, :] = hit_grad
    out[1:2, :] = per_row * weighted + hit_grad * hit_logit
    out[2:3, :] = hit_grad * scale[...]
    for n in range(count):
        out[4 + n : 5 + n, :] = per_row * by[n]
        out[4 + count + n : 5 + count + n, :] = per_row * by[n] * scale[...]


def input_grad_kernel(features, places, side, own, in_scale, grad_mixed, dots, *refs):
    came, (term, term_low) = refs[:-2], refs[-2:]
    width = side.shape[1]
    total = side[...]
    dot = dots[...]
    for each in came:
        total = total + each[:, :width].astype(f32)
        dot = dot + (
            each[:, width : width + 1].astype(f32) + each[:, width + 1 : width + 2].astype(f32)
        )
    normed = own[...].astype(f32) * in_scale[...]
    value = in_scale[...] * (total - normed * (dot / features))
    value = value + jnp.where(dp_at(places) == 0, grad_mixed[...], 0.0)
    term[...] = value
    term_low[...] = value.astype(bf16)


def fast_local(
    n_head,
    n_tensor,
    trunk_hidden,
    next_embeds,
    combine_weight,
    final_gain,
    unembed_weight,
    target_ids,
    loss_scale,
):
    half, width = trunk_hidden.shape
    rows = 2 * half
    features = width * n_tensor
    vocab_part = unembed_weight.shape[0]
    piece = vocab_part // n_tensor
    combine_whole, unembed_whole = combine_weight[0], unembed_weight
    weight_block = pltpu.with_memory_space_constraint(combine_weight[0], pltpu.HBM)
    unembed_weight = pltpu.with_memory_space_constraint(unembed_weight, pltpu.HBM)
    d = lax.axis_index("dp")
    t = lax.axis_index("tensor")
    h = lax.axis_index("head")
    first = d == 0
    places = (t + 16 * d).astype(jnp.int32).reshape(1)
    row_weights = loss_scale[0]

    def chunk_of(weight, r, size):
        return lax.dynamic_slice_in_dim(weight, (t ^ r) * size, size, 0)

    def spread(value):
        return [value] + [flip(value, "tensor", n_tensor, r) for r in range(1, n_tensor)]

    with jax.named_scope("inputs"):
        embeds = next_embeds[0]
        kept = jnp.where(first, trunk_hidden, embeds)
        given = jnp.where(first, embeds, trunk_hidden)
        kept_parts = spread(kept)
        swapped = swap(given)
        kept_parts, swapped = lax.optimization_barrier((kept_parts, swapped))
        given_parts = spread(swapped)
        trunk_other = swap(trunk_hidden)
        own, raw, squares = project_own(places, kept_parts[0], swapped, weight_block, 2)
        given_parts, trunk_other, own, raw, squares = lax.optimization_barrier(
            (given_parts, trunk_other, own, raw, squares)
        )
    with jax.named_scope("projection"):
        parts, projected, projected_low, in_scale = project(
            places, kept_parts[1:], given_parts[1:], weight_block, raw, squares, features, 2
        )
        projected_there = swap(projected_low)
        weight_far = chunk_of(unembed_whole, 3, piece)
        projected_there, weight_far = lax.optimization_barrier((projected_there, weight_far))
        trunk_rows = jnp.where(
            first, own, jnp.concatenate([trunk_other, trunk_hidden], axis=0)
        ).astype(f32)
        mixed = trunk_rows + (projected + projected_there.astype(f32))
        gained = mixed * final_gain[None, :]
        low = gained.astype(bf16)
    with jax.named_scope("logits"):
        (far,) = held_columns(places, low, [weight_far], f32)
        ends = lax.ppermute(far, "tensor", [(0, 1), (3, 2)])
        middle = lax.ppermute(far, "tensor", [(1, 2), (2, 1)])
        low_chips = [low, flip(low, "head", n_head, 2)]
        cross, near = stream_columns(places, low, unembed_weight, [2, 1], piece, 4, f32)
        wanted = (target_ids[0] - d * vocab_part)[:, None]
        squares = jnp.sum(mixed * mixed, axis=1)
        squares = jnp.stack([squares, flip(squares, "tensor", n_tensor, 1)])
        ends, middle, low_chips, cross, near, squares, wanted = lax.optimization_barrier(
            (ends, middle, low_chips, cross, near, squares, wanted)
        )
        low_cores = flip(jnp.stack(low_chips), "head", n_head, 1)
        squares_there = flip(squares, "tensor", n_tensor, 2)
        cross = flip(cross + ends, "tensor", n_tensor, 2)
        near = flip(near, "tensor", n_tensor, 1)
        chosen = lax.broadcasted_iota(jnp.int32, (1, vocab_part), 1) == wanted
        (target_rows,) = stream_rows(
            places, [chosen.astype(bf16)], unembed_weight, [None], 16, 8
        )
        (last,) = stream_columns(places, low_chips[0], unembed_weight, [0], piece, 4, f32)
        cross, near, low_cores, squares_there, target_rows, last = lax.optimization_barrier(
            (cross, near, low_cores, squares_there, target_rows, last)
        )
        low_heads = [low_chips[0], low_cores[0], low_chips[1], low_cores[1]]
        squares = squares[0] + squares[1] + squares_there[0] + squares_there[1]
        scale_row = lax.rsqrt(squares / features + epsilon)
        mixed_scale = scale_row[:, None]
        logits = (last + middle + cross + near) * mixed_scale
    with jax.named_scope("softmax"):
        hits = (lax.broadcasted_iota(jnp.int32, (1, piece), 1) + t * piece) == wanted
        top = jnp.max(logits, axis=1)
        shifted = jnp.exp(logits - top[:, None])
        shifted_low = jnp.where(hits, 0.0, shifted).astype(bf16)
        stats = jnp.stack(
            [
                top,
                jnp.sum(shifted, axis=1),
                jnp.sum(jnp.where(hits, logits, 0.0), axis=1),
                jnp.sum(shifted_low.astype(f32) * logits, axis=1),
            ]
        )
    with jax.named_scope("grad_normed"):
        cross = flip(shifted_low, "tensor", n_tensor, 2)
        near = flip(shifted_low, "tensor", n_tensor, 1)
        products = stream_rows(places, [shifted_low], unembed_weight, [0], 4, 4)
        stats, products = lax.optimization_barrier((stats, products))
        stats = spread(stats)
        weight_sent = [chunk_of(combine_whole, r, width) for r in (3, 2, 1)]
        weight_far = chunk_of(unembed_whole, 3, piece)
        cross, near, stats, products, value, weight_sent, weight_far = lax.optimization_barrier(
            (cross, near, stats, products, shifted_low, weight_sent, weight_far)
        )
        ends = lax.ppermute(cross, "tensor", [(2, 3), (1, 0)])
        middle = lax.ppermute(value, "tensor", [(1, 2), (2, 1)])
        stats = jnp.stack(stats)
        there = swap(stats)
        products += stream_rows(places, [near, cross], unembed_weight, [1, 2], 4, 8)
        ends, middle, there, products = lax.optimization_barrier((ends, middle, there, products))
        products += whole_call(
            held_between_kernel,
            places,
            [ends, middle, weight_far],
            [shaped(rows, width, f32)],
        )
        far = jnp.where((t == 0) | (t == n_tensor - 1), ends, middle)
        shifted_parts = [shifted_low, near, cross, far]
        (row_factors,) = whole_call(
            softmax_factors_kernel,
            places,
            [stats, there, row_weights[None, :], scale_row[None, :]],
            [shaped(4 + 2 * n_tensor, rows, f32)],
        )
        hit_grad, grad_dots, hit_scaled = row_factors[0], row_factors[1], row_factors[2]
        factors = [row_factors[4 + r] for r in range(n_tensor)]
        factors_scaled = [row_factors[4 + n_tensor + r] for r in range(n_tensor)]
        grad_part = hit_grad[:, None] * target_rows
        for r, product in enumerate(products):
            grad_part = grad_part + factors[r][:, None] * product
        grad_there = swap(grad_part.astype(bf16))
        ids = lax.broadcasted_iota(jnp.int32, (1, piece), 1)
        grad_stack = jnp.stack(
            [
                jnp.where(
                    (ids + (t ^ r) * piece) == wanted,
                    hit_scaled[:, None],
                    e.astype(f32) * factors_scaled[r][:, None],
                ).astype(bf16)
                for r, e in enumerate(shifted_parts)
            ]
        )
        grad_slices = [
            lax.dynamic_index_in_dim(grad_stack, t ^ h ^ m, 0, keepdims=False)
            for m in range(n_head)
        ]
        grad_there, grad_slices = lax.optimization_barrier((grad_there, grad_slices))
    with jax.named_scope("grad_mixed"):
        grad_normed = grad_part + grad_there.astype(f32)
        mixed_normed = mixed * mixed_scale
        grad_mixed = mixed_scale * (
            grad_normed * final_gain[None, :] - mixed_normed * (grad_dots / features)[:, None]
        )
        grad_low = grad_mixed.astype(bf16)
        grad_scaled = (in_scale * grad_mixed).astype(bf16)
        dots = jnp.sum(grad_low.astype(f32) * projected, axis=1, keepdims=True)
        dots_high = lax.reduce_precision(dots, 8, 7)
        lane = lax.broadcasted_iota(jnp.int32, (1, 128), 1)
        extra = jnp.where(
            lane == 0, dots_high, jnp.where(lane == 1, dots - dots_high, 0.0)
        ).astype(bf16)
    with jax.named_scope("joined_grad"):
        heads_near = flip(grad_slices[1], "head", n_head, 1)
        sent = held_columns(places, grad_low, weight_sent[:1], bf16, extra)
        heads_near, grad_low = lax.optimization_barrier((heads_near, grad_low))
        sent += held_columns(places, grad_low, weight_sent[1:], bf16, extra)
        came = [flip(c, "tensor", n_tensor, r) for r, c in zip((3, 2, 1), sent)]
        heads_given = [heads_near] + [
            flip(grad_slices[m], "head", n_head, m) for m in range(2, n_head)
        ]
        (side,) = stream_columns(places, grad_low, weight_block, [0], width, 2, f32)
        combine_grad = combine(places, own, parts, grad_scaled)[None]
        unembed_grad = head_sum([grad_slices[0]] + heads_given, low_heads, 2)
        unembed_grad = unembed_grad.reshape(1, 1, piece, width)
        came, side, combine_grad, unembed_grad = lax.optimization_barrier(
            (came, side, combine_grad, unembed_grad)
        )
    with jax.named_scope("input_grads"):
        term, term_low = whole_call(
            functools.partial(input_grad_kernel, features),
            places,
            [side, own, in_scale, grad_mixed, dots] + came,
            [shaped(rows, width, f32), shaped(rows, width, bf16)],
        )
        pair = flip(term_low, "head", n_head, 1)
        pair = term_low.astype(f32) + pair.astype(f32)
        pair_low = pair.astype(bf16)
        crossed = swap(jnp.where(first, pair_low[half:], term_low[:half]))
        beside = lax.ppermute(
            pair_low[:half], ("head", "dp"), [(2 * i, 2 * (i ^ 2)) for i in range(n_head)]
        )
        across = lax.ppermute(
            pair_low[half:], ("head", "dp"), [(2 * i, 2 * (i ^ 2) + 1) for i in range(n_head)]
        )
        crossed, beside, across = [v.astype(f32) for v in (crossed, beside, across)]
        embed_grad = jnp.where(first, crossed, term[half:])[None]
        trunk_grad = jnp.where(first, pair[:half] + beside, crossed + across)
    return (trunk_grad, embed_grad, combine_grad, unembed_grad)


def general_local(
    n_tensor,
    trunk_hidden,
    next_embeds,
    combine_weight,
    final_gain,
    unembed_weight,
    target_ids,
    loss_scale,
):
    rows, part_width = trunk_hidden.shape
    features = part_width * n_tensor
    vocab_part = unembed_weight.shape[0]
    weight_block = combine_weight[0]
    trunk_whole, embed_whole = (
        lax.all_gather(trunk_hidden, "tensor", axis=1, tiled=True),
        lax.all_gather(next_embeds[0], "tensor", axis=1, tiled=True),
    )
    trunk_float = trunk_whole.astype(f32)
    embed_float = embed_whole.astype(f32)
    trunk_scale = lax.rsqrt(jnp.sum(trunk_float * trunk_float, axis=1) / features + epsilon)
    embed_scale = lax.rsqrt(jnp.sum(embed_float * embed_float, axis=1) / features + epsilon)
    trunk_normed = trunk_float * trunk_scale[:, None]
    embed_normed = embed_float * embed_scale[:, None]
    joined = jnp.concatenate([trunk_normed.astype(bf16), embed_normed.astype(bf16)], axis=1)
    feature_start = lax.axis_index("tensor") * part_width
    trunk_local = lax.dynamic_slice_in_dim(trunk_normed, feature_start, part_width, 1)
    embed_local = lax.dynamic_slice_in_dim(embed_normed, feature_start, part_width, 1)
    blocks = lax.all_to_all(joined, "dp", split_axis=1, concat_axis=0, tiled=True)
    projected = lax.psum_scatter(
        plain_dot(blocks, weight_block).astype(bf16), "dp", scatter_dimension=0, tiled=True
    ).astype(f32)
    mixed = trunk_hidden.astype(f32) + projected
    mixed_sums = lax.psum(jnp.sum(mixed * mixed, axis=1), "tensor")
    mixed_scale = lax.rsqrt(mixed_sums / features + epsilon)
    mixed_normed = mixed * mixed_scale[:, None]
    normed_out = (mixed_normed * final_gain[None, :]).astype(bf16)
    normed_all = lax.all_gather(normed_out, "dp", axis=0, tiled=True)
    logits = lax.psum(contract_cols(normed_all, unembed_weight), "tensor")
    largest = lax.pmax(jnp.max(logits, axis=1), "dp")
    shifted = jnp.exp(logits - largest[:, None])
    summed = lax.psum(jnp.sum(shifted, axis=1), "dp")
    probs = shifted / summed[:, None]
    vocab_ids = (
        lax.broadcasted_iota(jnp.int32, (1, vocab_part), 1) + lax.axis_index("dp") * vocab_part
    )
    hits = (vocab_ids == target_ids[0][:, None]).astype(f32)
    grad_local = (loss_scale[0][:, None] * (probs - hits)).astype(bf16)
    grad_normed = lax.psum_scatter(
        plain_dot(grad_local, unembed_weight).astype(bf16), "dp", scatter_dimension=0, tiled=True
    ).astype(f32)
    vocab_term = contract_rows(grad_local, normed_all).astype(bf16)
    vocab_total = lax.psum_scatter(vocab_term, "head", scatter_dimension=0, tiled=True).astype(f32)
    unembed_grad = vocab_total.reshape(1, 1, vocab_total.shape[0], part_width)
    scaled_grad = grad_normed * final_gain[None, :]
    grad_dots = lax.psum(jnp.sum(scaled_grad * mixed_normed, axis=1), "tensor")
    grad_mixed = mixed_scale[:, None] * (
        scaled_grad - mixed_normed * (grad_dots / features)[:, None]
    )
    grad_all = lax.all_gather(grad_mixed.astype(bf16), "dp", axis=0, tiled=True)
    combine_grad = contract_rows(blocks, grad_all)[None]
    joined_part = lax.all_to_all(
        contract_cols(grad_all, weight_block).astype(bf16),
        "dp",
        split_axis=0,
        concat_axis=1,
        tiled=True,
    )
    joined_grad = lax.psum_scatter(
        joined_part.reshape(rows, 2, features), "tensor", scatter_dimension=2, tiled=True
    ).astype(f32)
    trunk_side = joined_grad[:, 0]
    embed_side = joined_grad[:, 1]
    trunk_dots, embed_dots = lax.psum(
        (jnp.sum(trunk_side * trunk_local, axis=1), jnp.sum(embed_side * embed_local, axis=1)),
        "tensor",
    )
    trunk_term = trunk_scale[:, None] * (
        trunk_side - trunk_local * (trunk_dots / features)[:, None]
    )
    embed_grad = (
        embed_scale[:, None] * (embed_side - embed_local * (embed_dots / features)[:, None])
    )[None]
    trunk_grad = lax.psum((grad_mixed + trunk_term).astype(bf16), "head").astype(f32)
    return (trunk_grad, embed_grad, combine_grad, unembed_grad)


def solution(mesh):
    n_head, n_tensor, n_dp = mesh.shape["head"], mesh.shape["tensor"], mesh.shape["dp"]
    in_specs = (
        P("dp", "tensor"),
        P("head", "dp", "tensor"),
        P("head", "dp", "tensor"),
        P("tensor"),
        P("dp", "tensor"),
        P("head", None),
        P("head", None),
    )
    out_specs = (
        P("dp", "tensor"),
        P("head", "dp", "tensor"),
        P("head", "dp", "tensor"),
        P("dp", "head", None, "tensor"),
    )
    if n_dp == 2 and n_tensor == 4 and n_head == 4:

        def local(*args):
            return fast_local(n_head, n_tensor, *args)

    else:

        def local(*args):
            return general_local(n_tensor, *args)

    return jax.shard_map(local, mesh=mesh, in_specs=in_specs, out_specs=out_specs, check_vma=False)
```

```python
import functools

import jax
import jax.numpy as jnp
from jax import lax
from jax.experimental import pallas as pl
from jax.experimental.pallas import tpu as pltpu
from jax.sharding import PartitionSpec as P

epsilon = 1e-05
f32 = jnp.float32
bf16 = jnp.bfloat16
kernel_memory = 16 << 20
brief = pl.CostEstimate(flops=0, bytes_accessed=0, transcendentals=0)
in_vmem = pl.BlockSpec(memory_space=pltpu.VMEM)
in_smem = pl.BlockSpec(memory_space=pltpu.SMEM)


def contract_rows(left, right):
    return lax.dot_general(
        left, right, (((0,), (0,)), ((), ())), preferred_element_type=f32
    )


def contract_cols(left, right):
    return lax.dot_general(
        left, right, (((1,), (1,)), ((), ())), preferred_element_type=f32
    )


def plain_dot(left, right):
    return jnp.dot(left, right, preferred_element_type=f32)


def flip(value, axis, size, mask):
    return lax.ppermute(value, axis, [(i, i ^ mask) for i in range(size)])


def swap(value):
    return lax.ppermute(value, "dp", [(0, 1), (1, 0)])


def params(memory):
    return pltpu.CompilerParams(vmem_limit_bytes=memory)


def shaped(*shape_and_type):
    *shape, dtype = shape_and_type
    return jax.ShapeDtypeStruct(tuple(shape), dtype)


def tensor_at(places):
    return places[0] % 16


def dp_at(places):
    return places[0] // 16


def whole_call(kernel, places, arrays, outs):
    return pl.pallas_call(
        kernel,
        out_shape=outs,
        in_specs=[in_smem] + [in_vmem] * len(arrays),
        out_specs=[in_vmem] * len(outs),
        compiler_params=params(kernel_memory),
        cost_estimate=brief,
    )(places, *arrays)


def join_rows(places, kept, given, put):
    half = kept.shape[0]

    @pl.when(dp_at(places) == 0)
    def _():
        put(slice(0, half), kept[...])
        put(slice(half, 2 * half), given[...])

    @pl.when(dp_at(places) != 0)
    def _():
        put(slice(0, half), given[...])
        put(slice(half, 2 * half), kept[...])


def column_block(j, block):
    return pl.ds(pl.multiple_of(j * block, 128), block)


def project_own_kernel(places, kept, given, weight, own, raw, squares):
    j = pl.program_id(0)

    @pl.when(j == 0)
    def _():
        def put(rows, value):
            own[rows] = value

        join_rows(places, kept, given, put)
        values = own[...].astype(f32)
        squares[...] = jnp.sum(values * values, axis=1, keepdims=True)
        raw[...] = jnp.zeros_like(raw)

    raw[...] += plain_dot(own[:, column_block(j, weight.shape[0])], weight[...])


def project_own(places, kept, given, weight, blocks):
    half, width = kept.shape
    rows = 2 * half
    fixed = lambda j, c: (0, 0)
    return pl.pallas_call(
        project_own_kernel,
        out_shape=[shaped(rows, width, bf16), shaped(rows, width, f32), shaped(rows, 1, f32)],
        grid_spec=pltpu.PrefetchScalarGridSpec(
            num_scalar_prefetch=1,
            grid=(blocks,),
            in_specs=[
                pl.BlockSpec((half, width), fixed),
                pl.BlockSpec((half, width), fixed),
                pl.BlockSpec((width // blocks, width), lambda j, c: (tensor_at(c) * blocks + j, 0)),
            ],
            out_specs=[
                pl.BlockSpec((rows, width), fixed),
                pl.BlockSpec((rows, width), fixed),
                pl.BlockSpec((rows, 1), fixed),
            ],
        ),
        compiler_params=params(kernel_memory),
        cost_estimate=brief,
    )(places, kept, given, weight)


def project_kernel(features, count, blocks, places, *refs):
    kept, given = refs[:count], refs[count : 2 * count]
    weight, raw, own_squares = refs[2 * count : 2 * count + 3]
    parts_out, projected, low, scale, parts, held, done, written = refs[2 * count + 3 :]
    writes = [
        pltpu.make_async_copy(parts.at[k], parts_out.at[k], written.at[k]) for k in range(count)
    ]
    squares = own_squares[...]
    total = projected
    chunks = list(range(1, count + 1))
    for n, right in streamed(places, weight, chunks, blocks, held, done):
        k, j = n // blocks, n % blocks
        block = right.shape[0]
        if j == 0:

            def put(rows, value, k=k):
                parts[k, rows] = value

            join_rows(places, kept[k], given[k], put)
            writes[k].start()
            values = parts[k].astype(f32)
            squares = squares + jnp.sum(values * values, axis=1, keepdims=True)
        product = plain_dot(parts[k, :, j * block : (j + 1) * block], right)
        total[...] = product + (raw[...] if n == 0 else total[...])
    scale[...] = lax.rsqrt(squares / features + epsilon)
    projected[...] = total[...] * scale[...]
    low[...] = projected[...].astype(bf16)
    for write in writes:
        write.wait()


def project(places, kept, given, weight, raw, squares, features, blocks):
    count = len(kept)
    half, width = kept[0].shape
    rows = 2 * half
    return pl.pallas_call(
        functools.partial(project_kernel, features, count, blocks),
        out_shape=[
            pltpu.HBM((count, rows, width), bf16),
            shaped(rows, width, f32),
            shaped(rows, width, bf16),
            shaped(rows, 1, f32),
        ],
        in_specs=[in_smem]
        + [in_vmem] * (2 * count)
        + [pl.BlockSpec(memory_space=pl.ANY), in_vmem, in_vmem],
        out_specs=[pl.BlockSpec(memory_space=pl.ANY)] + [in_vmem] * 3,
        scratch_shapes=[
            pltpu.VMEM((count, rows, width), bf16),
            pltpu.VMEM((count * blocks, width // blocks, width), weight.dtype),
            pltpu.SemaphoreType.DMA((count * blocks,)),
            pltpu.SemaphoreType.DMA((count,)),
        ],
        compiler_params=params(kernel_memory),
        cost_estimate=brief,
    )(places, *kept, *given, weight, raw, squares)


def held_columns_kernel(count, _, left, *refs):
    rights, extras, outs = refs[:count], refs[count:-count], refs[-count:]
    size = rights[0].shape[0]
    for right, out in zip(rights, outs):
        out[:, :size] = contract_cols(left[...], right[...]).astype(out.dtype)
        for extra in extras:
            out[:, size:] = extra[...]


def held_columns(places, left, rights, dtype, extra=None):
    extras = [] if extra is None else [extra]
    wide = rights[0].shape[0] + sum(e.shape[1] for e in extras)
    return whole_call(
        functools.partial(held_columns_kernel, len(rights)),
        places,
        [left] + rights + extras,
        [shaped(left.shape[0], wide, dtype) for _ in rights],
    )


def held_between_kernel(places, outer, inner, right, out):
    t = tensor_at(places)
    at_end = (t == 0) | (t == 3)

    @pl.when(at_end)
    def _():
        out[...] = plain_dot(outer[...], right[...])

    @pl.when(jnp.logical_not(at_end))
    def _():
        out[...] = plain_dot(inner[...], right[...])


def streamed(places, weight, chunks, blocks, held, done):
    slots, block, _ = held.shape
    copies = []
    for n in range(blocks * len(chunks)):
        start = (n % blocks) * block
        if chunks[n // blocks] is not None:
            place = tensor_at(places) ^ chunks[n // blocks]
            start = pl.multiple_of(place * (blocks * block) + start, block)
        slot = n % slots
        copies.append(
            pltpu.make_async_copy(weight.at[pl.ds(start, block)], held.at[slot], done.at[slot])
        )
    for copy in copies[:slots]:
        copy.start()
    for n, copy in enumerate(copies):
        copy.wait()
        yield n, held[n % slots]
        if n + slots < len(copies):
            copies[n + slots].start()


def stream_columns_kernel(chunks, blocks, places, left, weight, *refs):
    outs, (held, done) = refs[:-2], refs[-2:]
    block = held.shape[1]
    for n, right in streamed(places, weight, chunks, blocks, held, done):
        j = n % blocks
        product = contract_cols(left[...], right)
        outs[n // blocks][:, j * block : (j + 1) * block] = product.astype(outs[0].dtype)


def stream_rows_kernel(chunks, blocks, places, *refs):
    count = len(chunks)
    sources, weight, outs = refs[:count], refs[count], refs[count + 1 : 2 * count + 1]
    held, done, lefts, fetched = refs[2 * count + 1 :]
    fetches = [
        pltpu.make_async_copy(source, lefts.at[k], fetched.at[k])
        for k, source in enumerate(sources)
    ]
    for fetch in fetches:
        fetch.start()
    block = held.shape[1]
    for n, right in streamed(places, weight, chunks, blocks, held, done):
        k, j = n // blocks, n % blocks
        if j == 0:
            fetches[k].wait()
        product = plain_dot(lefts[k, :, j * block : (j + 1) * block], right)
        if j == 0:
            outs[k][...] = product
        else:
            outs[k][...] += product


def stream(kernel, places, lefts, weight, chunks, size, outs, blocks, slots):
    return pl.pallas_call(
        functools.partial(kernel, chunks, blocks),
        out_shape=outs,
        in_specs=[in_smem] + [in_vmem] * len(lefts) + [pl.BlockSpec(memory_space=pl.ANY)],
        out_specs=[in_vmem] * len(outs),
        scratch_shapes=[
            pltpu.VMEM((slots, size // blocks, weight.shape[1]), weight.dtype),
            pltpu.SemaphoreType.DMA((slots,)),
        ],
        compiler_params=params(kernel_memory),
        cost_estimate=brief,
    )(places, *lefts, weight)


def stream_columns(places, left, weight, chunks, size, blocks, dtype):
    outs = [shaped(left.shape[0], size, dtype) for _ in chunks]
    slots = blocks * len(chunks)
    return stream(
        stream_columns_kernel, places, [left], weight, chunks, size, outs, blocks, slots
    )


def stream_rows(places, lefts, weight, chunks, blocks, slots):
    rows, size = lefts[0].shape
    count = len(chunks)
    outs = [shaped(rows, weight.shape[1], f32) for _ in chunks]
    anywhere = pl.BlockSpec(memory_space=pl.ANY)
    return pl.pallas_call(
        functools.partial(stream_rows_kernel, chunks, blocks),
        out_shape=outs,
        in_specs=[in_smem] + [anywhere] * (count + 1),
        out_specs=[in_vmem] * count,
        scratch_shapes=[
            pltpu.VMEM((slots, size // blocks, weight.shape[1]), weight.dtype),
            pltpu.SemaphoreType.DMA((slots,)),
            pltpu.VMEM((count, rows, size), bf16),
            pltpu.SemaphoreType.DMA((count,)),
        ],
        compiler_params=params(kernel_memory),
        cost_estimate=brief,
    )(places, *lefts, weight)


def combine_kernel(places, own, part, grad, out):
    c = pl.program_id(0)

    @pl.when(tensor_at(places) == c)
    def _():
        out[...] = contract_rows(own[...], grad[...])

    @pl.when(tensor_at(places) != c)
    def _():
        out[...] = contract_rows(part[0], grad[...])


def combine(places, own, parts, grad):
    rows, width = own.shape
    count = parts.shape[0] + 1
    fixed = lambda c, w: (0, 0)
    return pl.pallas_call(
        combine_kernel,
        out_shape=shaped(count * width, grad.shape[1], f32),
        grid_spec=pltpu.PrefetchScalarGridSpec(
            num_scalar_prefetch=1,
            grid=(count,),
            in_specs=[
                pl.BlockSpec((rows, width), fixed),
                pl.BlockSpec(
                    (1, rows, width), lambda c, w: (jnp.maximum((tensor_at(w) ^ c) - 1, 0), 0, 0)
                ),
                pl.BlockSpec((rows, grad.shape[1]), fixed),
            ],
            out_specs=pl.BlockSpec((width, grad.shape[1]), lambda c, w: (c, 0)),
        ),
        compiler_params=params(kernel_memory),
        cost_estimate=brief,
    )(places, own, parts, grad)


def head_sum_kernel(count, *refs):
    out = refs[-1]
    left = jnp.concatenate([r[...] for r in refs[:count]], axis=0)
    right = jnp.concatenate([r[...] for r in refs[count : 2 * count]], axis=0)
    out[...] = contract_rows(left, right)


def head_sum(grads, normed, blocks, half, base=None):
    rows, size = grads[0].shape
    width = normed[0].shape[1]
    block = size // blocks
    start = half * blocks // 2
    based = [] if base is None else [base]
    return pl.pallas_call(
        functools.partial(head_sum_kernel, len(grads)),
        out_shape=shaped(size, width, f32),
        grid=(blocks // 2,),
        in_specs=[pl.BlockSpec((rows, block), lambda j: (0, start + j))] * len(grads)
        + [pl.BlockSpec((rows, width), lambda j: (0, 0))] * len(normed)
        + [pl.BlockSpec(memory_space=pl.ANY)] * len(based),
        out_specs=pl.BlockSpec((block, width), lambda j: (start + j, 0)),
        input_output_aliases={} if base is None else {2 * len(grads): 0},
        compiler_params=params(kernel_memory),
        cost_estimate=brief,
    )(*grads, *normed, *based)


def softmax_factors_kernel(_, here, there, weights, scale, out):
    count = here.shape[0]
    shards = [[r[n, k : k + 1, :] for k in range(4)] for r in (here, there) for n in range(count)]
    largest = shards[0][0]
    for shard in shards[1:]:
        largest = jnp.maximum(largest, shard[0])
    by = [jnp.exp(shard[0] - largest) for shard in shards]
    summed = sum(shard[1] * b for shard, b in zip(shards, by))
    hit_logit = sum(shard[2] for shard in shards)
    weighted = sum(shard[3] * b for shard, b in zip(shards, by))
    per_row = weights[...] / summed
    hit_grad = weights[...] * (jnp.exp(hit_logit - largest) / summed - 1.0)
    out[0:1, :] = hit_grad
    out[1:2, :] = per_row * weighted + hit_grad * hit_logit
    out[2:3, :] = hit_grad * scale[...]
    for n in range(count):
        out[4 + n : 5 + n, :] = per_row * by[n]
        out[4 + count + n : 5 + count + n, :] = per_row * by[n] * scale[...]


def input_grad_kernel(features, places, side, own, in_scale, grad_mixed, dots, *refs):
    came, (term, term_low) = refs[:-2], refs[-2:]
    width = side.shape[1]
    total = side[...]
    dot = dots[...]
    for each in came:
        total = total + each[:, :width].astype(f32)
        dot = dot + (
            each[:, width : width + 1].astype(f32) + each[:, width + 1 : width + 2].astype(f32)
        )
    normed = own[...].astype(f32) * in_scale[...]
    value = in_scale[...] * (total - normed * (dot / features))
    value = value + jnp.where(dp_at(places) == 0, grad_mixed[...], 0.0)
    term[...] = value
    term_low[...] = value.astype(bf16)


def fast_local(
    n_head,
    n_tensor,
    trunk_hidden,
    next_embeds,
    combine_weight,
    final_gain,
    unembed_weight,
    target_ids,
    loss_scale,
):
    half, width = trunk_hidden.shape
    rows = 2 * half
    features = width * n_tensor
    vocab_part = unembed_weight.shape[0]
    piece = vocab_part // n_tensor
    combine_whole, unembed_whole = combine_weight[0], unembed_weight
    weight_block = pltpu.with_memory_space_constraint(combine_weight[0], pltpu.HBM)
    unembed_weight = pltpu.with_memory_space_constraint(unembed_weight, pltpu.HBM)
    d = lax.axis_index("dp")
    t = lax.axis_index("tensor")
    h = lax.axis_index("head")
    first = d == 0
    places = (t + 16 * d).astype(jnp.int32).reshape(1)
    row_weights = loss_scale[0]

    def chunk_of(weight, r, size):
        return lax.dynamic_slice_in_dim(weight, (t ^ r) * size, size, 0)

    def spread(value):
        return [value] + [flip(value, "tensor", n_tensor, r) for r in range(1, n_tensor)]

    with jax.named_scope("inputs"):
        embeds = next_embeds[0]
        kept = jnp.where(first, trunk_hidden, embeds)
        given = jnp.where(first, embeds, trunk_hidden)
        kept_parts = spread(kept)
        swapped = swap(given)
        kept_parts, swapped = lax.optimization_barrier((kept_parts, swapped))
        given_parts = spread(swapped)
        trunk_other = swap(trunk_hidden)
        own, raw, squares = project_own(places, kept_parts[0], swapped, weight_block, 2)
        given_parts, trunk_other, own, raw, squares = lax.optimization_barrier(
            (given_parts, trunk_other, own, raw, squares)
        )
    with jax.named_scope("projection"):
        parts, projected, projected_low, in_scale = project(
            places, kept_parts[1:], given_parts[1:], weight_block, raw, squares, features, 2
        )
        projected_there = swap(projected_low)
        weight_far = chunk_of(unembed_whole, 3, piece)
        projected_there, weight_far = lax.optimization_barrier((projected_there, weight_far))
        trunk_rows = jnp.where(
            first, own, jnp.concatenate([trunk_other, trunk_hidden], axis=0)
        ).astype(f32)
        mixed = trunk_rows + (projected + projected_there.astype(f32))
        gained = mixed * final_gain[None, :]
        low = gained.astype(bf16)
    with jax.named_scope("logits"):
        (far,) = held_columns(places, low, [weight_far], f32)
        ends = lax.ppermute(far, "tensor", [(0, 1), (3, 2)])
        middle = lax.ppermute(far, "tensor", [(1, 2), (2, 1)])
        low_chips = [low, flip(low, "head", n_head, 2)]
        cross, near = stream_columns(places, low, unembed_weight, [2, 1], piece, 4, f32)
        wanted = (target_ids[0] - d * vocab_part)[:, None]
        squares = jnp.sum(mixed * mixed, axis=1)
        squares = jnp.stack([squares, flip(squares, "tensor", n_tensor, 1)])
        ends, middle, low_chips, cross, near, squares, wanted = lax.optimization_barrier(
            (ends, middle, low_chips, cross, near, squares, wanted)
        )
        low_cores = flip(jnp.stack(low_chips), "head", n_head, 1)
        squares_there = flip(squares, "tensor", n_tensor, 2)
        cross = flip(cross + ends, "tensor", n_tensor, 2)
        near = flip(near, "tensor", n_tensor, 1)
        chosen = lax.broadcasted_iota(jnp.int32, (1, vocab_part), 1) == wanted
        (target_rows,) = stream_rows(
            places, [chosen.astype(bf16)], unembed_weight, [None], 8, 4
        )
        (last,) = stream_columns(places, low_chips[0], unembed_weight, [0], piece, 4, f32)
        cross, near, low_cores, squares_there, target_rows, last, scale_in = (
            lax.optimization_barrier(
                (cross, near, low_cores, squares_there, target_rows, last, in_scale[:, 0])
            )
        )
        low_heads = [low_chips[0], low_cores[0], low_chips[1], low_cores[1]]
        squares = squares[0] + squares[1] + squares_there[0] + squares_there[1]
        scale_row = lax.rsqrt(squares / features + epsilon)
        mixed_scale = scale_row[:, None]
        logits = (last + middle + cross + near) * mixed_scale
    with jax.named_scope("softmax"):
        hits = (lax.broadcasted_iota(jnp.int32, (1, piece), 1) + t * piece) == wanted
        top = jnp.max(logits, axis=1)
        shifted = jnp.exp(logits - top[:, None])
        shifted_low = jnp.where(hits, 0.0, shifted).astype(bf16)
        stats = jnp.stack(
            [
                top,
                jnp.sum(shifted, axis=1),
                jnp.sum(jnp.where(hits, logits, 0.0), axis=1),
                jnp.sum(shifted_low.astype(f32) * logits, axis=1),
            ]
        )
    with jax.named_scope("grad_normed"):
        cross = flip(shifted_low, "tensor", n_tensor, 2)
        near = flip(shifted_low, "tensor", n_tensor, 1)
        products = stream_rows(places, [shifted_low], unembed_weight, [0], 2, 2)
        stats, products = lax.optimization_barrier((stats, products))
        stats = spread(stats)
        weight_sent = [chunk_of(combine_whole, r, width) for r in (3, 2, 1)]
        weight_far = chunk_of(unembed_whole, 3, piece)
        cross, near, stats, products, value, weight_sent, weight_far = lax.optimization_barrier(
            (cross, near, stats, products, shifted_low, weight_sent, weight_far)
        )
        ends = lax.ppermute(cross, "tensor", [(2, 3), (1, 0)])
        middle = lax.ppermute(value, "tensor", [(1, 2), (2, 1)])
        stats = jnp.stack(stats)
        there = swap(stats)
        products += stream_rows(places, [near, cross], unembed_weight, [1, 2], 2, 4)
        ends, middle, there, products, wanted = lax.optimization_barrier(
            (ends, middle, there, products, wanted)
        )
        products += whole_call(
            held_between_kernel,
            places,
            [ends, middle, weight_far],
            [shaped(rows, width, f32)],
        )
        far = jnp.where((t == 0) | (t == n_tensor - 1), ends, middle)
        shifted_parts = [shifted_low, near, cross, far]
        (row_factors,) = whole_call(
            softmax_factors_kernel,
            places,
            [stats, there, row_weights[None, :], scale_row[None, :]],
            [shaped(4 + 2 * n_tensor, rows, f32)],
        )
        hit_grad, grad_dots, hit_scaled = row_factors[0], row_factors[1], row_factors[2]
        factors = [row_factors[4 + r] for r in range(n_tensor)]
        factors_scaled = [row_factors[4 + n_tensor + r] for r in range(n_tensor)]
        grad_part = hit_grad[:, None] * target_rows
        for r, product in enumerate(products):
            grad_part = grad_part + factors[r][:, None] * product
        grad_there = swap(grad_part.astype(bf16))
        ids = lax.broadcasted_iota(jnp.int32, (1, piece), 1)
        grad_stack = jnp.stack(
            [
                jnp.where(
                    ids == wanted - (t ^ r) * piece,
                    hit_scaled[:, None],
                    e.astype(f32) * factors_scaled[r][:, None],
                ).astype(bf16)
                for r, e in enumerate(shifted_parts)
            ]
        )
        grad_slices = [
            lax.dynamic_index_in_dim(grad_stack, t ^ h ^ m, 0, keepdims=False)
            for m in range(n_head)
        ]
        grad_there, grad_slices = lax.optimization_barrier((grad_there, grad_slices))
    with jax.named_scope("grad_mixed"):
        grad_normed = grad_part + grad_there.astype(f32)
        mixed_normed = mixed * mixed_scale
        grad_mixed = mixed_scale * (
            grad_normed * final_gain[None, :] - mixed_normed * (grad_dots / features)[:, None]
        )
        grad_low = grad_mixed.astype(bf16)
        grad_scaled = (scale_in[:, None] * grad_mixed).astype(bf16)
        dots = jnp.sum(grad_low.astype(f32) * projected, axis=1, keepdims=True)
        dots_high = lax.reduce_precision(dots, 8, 7)
        lane = lax.broadcasted_iota(jnp.int32, (1, 128), 1)
        extra = jnp.where(
            lane == 0, dots_high, jnp.where(lane == 1, dots - dots_high, 0.0)
        ).astype(bf16)
    with jax.named_scope("joined_grad"):
        heads_near = flip(grad_slices[1], "head", n_head, 1)
        sent = held_columns(places, grad_low, weight_sent[:1], bf16, extra)
        heads_near, grad_low = lax.optimization_barrier((heads_near, grad_low))
        sent += held_columns(places, grad_low, weight_sent[1:], bf16, extra)
        came = [flip(c, "tensor", n_tensor, r) for r, c in zip((3, 2, 1), sent)]
        heads_given = [heads_near] + [
            flip(grad_slices[m], "head", n_head, m) for m in range(2, n_head)
        ]
        (side,) = stream_columns(places, grad_low, weight_block, [0], width, 2, f32)
        combine_grad = combine(places, own, parts, grad_scaled)[None]
        came, side, combine_grad = lax.optimization_barrier((came, side, combine_grad))
    with jax.named_scope("input_grads"):
        term, term_low = whole_call(
            functools.partial(input_grad_kernel, features),
            places,
            [side, own, in_scale, grad_mixed, dots] + came,
            [shaped(rows, width, f32), shaped(rows, width, bf16)],
        )
        crossed = swap(jnp.where(first, term_low[half:], term_low[:half]))
        heads = [grad_slices[0]] + heads_given
        unembed_grad = head_sum(heads, low_heads, 4, 0)
        crossed, unembed_grad = lax.optimization_barrier((crossed, unembed_grad))
        crossed = crossed.astype(f32)
        embed_grad = jnp.where(first, crossed, term[half:])[None]
        trunk = jnp.where(first, term[:half], crossed)
        trunk_low = trunk.astype(bf16)
        core = flip(trunk_low, "head", n_head, 1)
        core, unembed_grad = lax.optimization_barrier((core, unembed_grad))
        trunk_low = (trunk_low.astype(f32) + core.astype(f32)).astype(bf16)
        over = flip(trunk_low, "head", n_head, 2)
        unembed_grad = head_sum(heads, low_heads, 4, 1, unembed_grad)
        over, unembed_grad = lax.optimization_barrier((over, unembed_grad))
        trunk_grad = trunk_low.astype(f32) + over.astype(f32)
        unembed_grad = unembed_grad.reshape(1, 1, piece, width)
    return (trunk_grad, embed_grad, combine_grad, unembed_grad)


def general_local(
    n_tensor,
    trunk_hidden,
    next_embeds,
    combine_weight,
    final_gain,
    unembed_weight,
    target_ids,
    loss_scale,
):
    rows, part_width = trunk_hidden.shape
    features = part_width * n_tensor
    vocab_part = unembed_weight.shape[0]
    weight_block = combine_weight[0]
    trunk_whole, embed_whole = (
        lax.all_gather(trunk_hidden, "tensor", axis=1, tiled=True),
        lax.all_gather(next_embeds[0], "tensor", axis=1, tiled=True),
    )
    trunk_float = trunk_whole.astype(f32)
    embed_float = embed_whole.astype(f32)
    trunk_scale = lax.rsqrt(jnp.sum(trunk_float * trunk_float, axis=1) / features + epsilon)
    embed_scale = lax.rsqrt(jnp.sum(embed_float * embed_float, axis=1) / features + epsilon)
    trunk_normed = trunk_float * trunk_scale[:, None]
    embed_normed = embed_float * embed_scale[:, None]
    joined = jnp.concatenate([trunk_normed.astype(bf16), embed_normed.astype(bf16)], axis=1)
    feature_start = lax.axis_index("tensor") * part_width
    trunk_local = lax.dynamic_slice_in_dim(trunk_normed, feature_start, part_width, 1)
    embed_local = lax.dynamic_slice_in_dim(embed_normed, feature_start, part_width, 1)
    blocks = lax.all_to_all(joined, "dp", split_axis=1, concat_axis=0, tiled=True)
    projected = lax.psum_scatter(
        plain_dot(blocks, weight_block).astype(bf16), "dp", scatter_dimension=0, tiled=True
    ).astype(f32)
    mixed = trunk_hidden.astype(f32) + projected
    mixed_sums = lax.psum(jnp.sum(mixed * mixed, axis=1), "tensor")
    mixed_scale = lax.rsqrt(mixed_sums / features + epsilon)
    mixed_normed = mixed * mixed_scale[:, None]
    normed_out = (mixed_normed * final_gain[None, :]).astype(bf16)
    normed_all = lax.all_gather(normed_out, "dp", axis=0, tiled=True)
    logits = lax.psum(contract_cols(normed_all, unembed_weight), "tensor")
    largest = lax.pmax(jnp.max(logits, axis=1), "dp")
    shifted = jnp.exp(logits - largest[:, None])
    summed = lax.psum(jnp.sum(shifted, axis=1), "dp")
    probs = shifted / summed[:, None]
    vocab_ids = (
        lax.broadcasted_iota(jnp.int32, (1, vocab_part), 1) + lax.axis_index("dp") * vocab_part
    )
    hits = (vocab_ids == target_ids[0][:, None]).astype(f32)
    grad_local = (loss_scale[0][:, None] * (probs - hits)).astype(bf16)
    grad_normed = lax.psum_scatter(
        plain_dot(grad_local, unembed_weight).astype(bf16), "dp", scatter_dimension=0, tiled=True
    ).astype(f32)
    vocab_term = contract_rows(grad_local, normed_all).astype(bf16)
    vocab_total = lax.psum_scatter(vocab_term, "head", scatter_dimension=0, tiled=True).astype(f32)
    unembed_grad = vocab_total.reshape(1, 1, vocab_total.shape[0], part_width)
    scaled_grad = grad_normed * final_gain[None, :]
    grad_dots = lax.psum(jnp.sum(scaled_grad * mixed_normed, axis=1), "tensor")
    grad_mixed = mixed_scale[:, None] * (
        scaled_grad - mixed_normed * (grad_dots / features)[:, None]
    )
    grad_all = lax.all_gather(grad_mixed.astype(bf16), "dp", axis=0, tiled=True)
    combine_grad = contract_rows(blocks, grad_all)[None]
    joined_part = lax.all_to_all(
        contract_cols(grad_all, weight_block).astype(bf16),
        "dp",
        split_axis=0,
        concat_axis=1,
        tiled=True,
    )
    joined_grad = lax.psum_scatter(
        joined_part.reshape(rows, 2, features), "tensor", scatter_dimension=2, tiled=True
    ).astype(f32)
    trunk_side = joined_grad[:, 0]
    embed_side = joined_grad[:, 1]
    trunk_dots, embed_dots = lax.psum(
        (jnp.sum(trunk_side * trunk_local, axis=1), jnp.sum(embed_side * embed_local, axis=1)),
        "tensor",
    )
    trunk_term = trunk_scale[:, None] * (
        trunk_side - trunk_local * (trunk_dots / features)[:, None]
    )
    embed_grad = (
        embed_scale[:, None] * (embed_side - embed_local * (embed_dots / features)[:, None])
    )[None]
    trunk_grad = lax.psum((grad_mixed + trunk_term).astype(bf16), "head").astype(f32)
    return (trunk_grad, embed_grad, combine_grad, unembed_grad)


def solution(mesh):
    n_head, n_tensor, n_dp = mesh.shape["head"], mesh.shape["tensor"], mesh.shape["dp"]
    in_specs = (
        P("dp", "tensor"),
        P("head", "dp", "tensor"),
        P("head", "dp", "tensor"),
        P("tensor"),
        P("dp", "tensor"),
        P("head", None),
        P("head", None),
    )
    out_specs = (
        P("dp", "tensor"),
        P("head", "dp", "tensor"),
        P("head", "dp", "tensor"),
        P("dp", "head", None, "tensor"),
    )
    if n_dp == 2 and n_tensor == 4 and n_head == 4:

        def local(*args):
            return fast_local(n_head, n_tensor, *args)

    else:

        def local(*args):
            return general_local(n_tensor, *args)

    return jax.shard_map(local, mesh=mesh, in_specs=in_specs, out_specs=out_specs, check_vma=False)
```
